128 devices in a mesh: grp: 4 (over z), gx: 32 (over y, x, core).
Axes of the slice: x: 4, y: 4, z: 4, core: 2. Of those that a mesh axis runs over, the one named last changes fastest.
Arguments:
- component_density: float32 [53, 1024, 1024], P(None, 'gx', 'grp'), may hold values from 0.05 to 2
- scaled_thermal_state: float32 [1024, 1024], P('gx', 'grp'), may hold values from 0.5 to 1.5
- leading_direction_flow: float32 [1024, 1024], P('gx', 'grp'), may hold values from -1 to 1
- trailing_direction_flow: float32 [1024, 1024], P('gx', 'grp'), may hold values from -1 to 1
- spreading_coefficient: float32 [54], replicated, may hold values from 0.02 to 0.2
- colliding_pair: int32 [325, 2], replicated, may hold values from 0 to 52
- natural_exponent_scaler: float32 [325], replicated, may hold values from -3 to -1
- arrhenius_energy: float32 [325], replicated, may hold values from 0 to 2
- stoichiometric_output: float32 [325, 53], replicated, may hold values from 0.004 to 0.075
- formation_warming: float32 [53], replicated, may hold values from -1.8 to 1.8
- explicit_increments: int32 [8192], P(('grp', 'gx')), may hold values from 1 to 4, as said below
Outputs:
- species_out: float32 [53, 1024, 1024], P(None, 'gx', 'grp')
- temperature_out: float32 [1024, 1024], P('gx', 'grp')
The draws below stay inside these ranges and needn't reach their ends.
Inputs may be any that keep to these rules, and one draw needn't show every extreme that they name: `explicit_increments`: substep counts of the tiles, in the order of the tiles described in the reference program.
All inputs are finite; a program needn't handle non-finite values.
Results may differ from the reference program's by a relative error of at most 0.0003.
Values sent between devices are 32-bit elements; how exact they have to be, the bound alone decides.
No kernel may reach another device: no remote copies, remote signals or barrier semaphores. Data moves between devices by JAX's collectives and lax.ppermute only.
A program may use at most 64 MiB of HBM per device.

```python
import math
import jax
import jax.numpy as jnp
from jax import lax

SPEC = 53
RXN = 325
CX = 32
CY = 256
TILE = 128
MINSUB = 1
MAXSUB = 4
GRID_LENGTH_LEAD = 1024
GRID_LENGTH_TRAIL = 1024
TD = 64
TILES = 8192
N_GRP = 4
N_GX = 32


def draw_explicit_increments(key, part):
    device_count = TILES // TD
    hot_key, drawn_key, busy_key, place_key = jax.random.split(key, 4)
    heated = jax.random.randint(hot_key, (device_count, 1), 0, 8) == 0
    drawn = jax.random.randint(drawn_key, (device_count, TD), MINSUB, MINSUB + 2)
    busy = jax.random.randint(busy_key, (device_count, TD), MAXSUB - 1, MAXSUB + 1)
    tallies = jnp.where(heated, busy, drawn).reshape(TILES)
    spots = jax.random.randint(place_key, (1,), 0, TILES)
    tallies = tallies.at[spots[0]].set(MAXSUB)
    other_spot = (spots[0] + TD) % TILES
    tallies = tallies.at[other_spot].set(MINSUB)
    return tallies.astype(jnp.int32)


def touch_ends(values, stream_key, smallest, high):
    longest = values.shape.index(max(values.shape))
    spots = []
    for shift in (0, 1):
        where = [jax.random.randint(jax.random.fold_in(stream_key, axis), (), 0, length) for axis, length in enumerate(values.shape)]
        where[longest] = (where[longest] + shift) % values.shape[longest]
        spots.append(tuple(where))
    return values.at[spots[0]].set(smallest).at[spots[1]].set(high)


def levels(own_key, dims, pieces, low, largest):
    loudness, own = 1.0, jax.random.fold_in(own_key, 6)
    for axis_at, blocks in pieces:
        heights = jnp.exp(jax.random.uniform(jax.random.fold_in(own, axis_at), (blocks,), jnp.float32, low / len(pieces), largest / len(pieces)))
        loudness = loudness * jnp.repeat(heights, dims[axis_at] // blocks).reshape([-1 if axis == axis_at else 1 for axis in range(len(dims))])
    return loudness


def normal_values(stream_key, shape, scale, limit, held_as=jnp.bfloat16):
    array = scale * jax.random.normal(stream_key, shape, jnp.float32)
    return jnp.clip(array, min=-limit, max=limit).astype(held_as)


def setup_inputs(seed: int = 0) -> dict:
    splits = jax.random.split(jax.random.key(seed), 12)
    return {
        "component_density": jnp.clip(jnp.exp(math.log(2.0) - 3.6888794 * jax.random.uniform(splits[0], (SPEC, GRID_LENGTH_LEAD, GRID_LENGTH_TRAIL), jnp.float32) ** levels(splits[0], (SPEC, GRID_LENGTH_LEAD, GRID_LENGTH_TRAIL), ((1, 32), (2, 4)), -0.2, 0.2)), 0.05, 2.0),
        "scaled_thermal_state": jnp.clip(0.5 + 1.0 * jax.random.uniform(splits[1], (GRID_LENGTH_LEAD, GRID_LENGTH_TRAIL), jnp.float32) ** levels(splits[1], (GRID_LENGTH_LEAD, GRID_LENGTH_TRAIL), ((0, 32), (1, 4)), -0.2, 0.2), 0.5, 1.5),
        "leading_direction_flow": jnp.clip(jax.random.uniform(splits[2], (GRID_LENGTH_LEAD, GRID_LENGTH_TRAIL), jnp.float32, -1.0, 1.0) * levels(splits[2], (GRID_LENGTH_LEAD, GRID_LENGTH_TRAIL), ((0, 32), (1, 4)), -0.4, 0.0), -1.0, 1.0),
        "trailing_direction_flow": jnp.clip(jax.random.uniform(splits[3], (GRID_LENGTH_LEAD, GRID_LENGTH_TRAIL), jnp.float32, -1.0, 1.0) * levels(splits[3], (GRID_LENGTH_LEAD, GRID_LENGTH_TRAIL), ((0, 32), (1, 4)), -0.4, 0.0), -1.0, 1.0),
        "spreading_coefficient": jnp.clip(jnp.exp(jax.random.uniform(splits[4], (SPEC + 1,), jnp.float32, math.log(0.02), math.log(0.2))), 0.02, 0.2),
        "colliding_pair": touch_ends(jax.random.randint(splits[5], (RXN, 2), 0, SPEC), jax.random.fold_in(splits[5], 1), 0, SPEC - 1).astype(jnp.int32),
        "natural_exponent_scaler": jnp.clip(jax.random.uniform(splits[6], (RXN,), jnp.float32, -3.0, -1.0), -3.0, -1.0),
        "arrhenius_energy": jnp.clip(jax.random.uniform(splits[7], (RXN,), jnp.float32, 0.0, 2.0), 0.0, 2.0),
        "stoichiometric_output": jnp.clip(jnp.exp(jax.random.uniform(splits[8], (RXN, SPEC), jnp.float32, math.log(0.004), math.log(0.075))), 0.004, 0.075),
        "formation_warming": normal_values(splits[9], (SPEC,), 0.3, 1.8, jnp.float32),
        "explicit_increments": draw_explicit_increments(jax.random.fold_in(splits[11], 71), 0),
    }


transport_step = 0.4
chemistry_span = 0.5
sixth_first = (0.75, -0.15, 1.0 / 60.0)
sixth_second = (1.5, -0.15, 1.0 / 90.0)
sixth_center = -49.0 / 18.0


def tendency(extended, speeds, spreading_coefficient):
    height = extended.shape[1] - 6
    breadth = extended.shape[2] - 6

    def along_first(values, offset):
        return values[:, 3 + offset:3 + offset + height, 3:3 + breadth]

    def along_second(values, offset):
        return values[:, 3:3 + height, 3 + offset:3 + offset + breadth]

    east_flux = speeds[0:1] * extended
    north_flux = speeds[1:2] * extended
    gradient = jnp.zeros((extended.shape[0], height, breadth), jnp.float32)
    laplacian = 2.0 * sixth_center * along_first(extended, 0)
    for offset in range(1, 4):
        gradient = gradient + sixth_first[offset - 1] * (along_first(east_flux, offset) - along_first(east_flux, -offset) + along_second(north_flux, offset) - along_second(north_flux, -offset))
        laplacian = laplacian + sixth_second[offset - 1] * (along_first(extended, offset) + along_first(extended, -offset) + along_second(extended, offset) + along_second(extended, -offset))
    return spreading_coefficient[:, None, None] * laplacian - gradient


def build_tables(colliding_pair, stoichiometric_output):
    species_ids = jnp.arange(stoichiometric_output.shape[1], dtype=jnp.int32)[:, None]
    first_table = (species_ids == colliding_pair[None, :, 0]).astype(jnp.float32)
    second_table = (species_ids == colliding_pair[None, :, 1]).astype(jnp.float32)
    return stoichiometric_output.T, jnp.concatenate([first_table, second_table], 1)


def substep_once(combined_state_array, step_sizes, mechanism):
    gain_table, loss_table, colliding_pair, natural_exponent_scaler, arrhenius_energy, formation_warming = mechanism
    amounts = combined_state_array[:-1]
    warmth = combined_state_array[-1]
    rate_constant = jnp.exp(natural_exponent_scaler[:, None] + arrhenius_energy[:, None] * jnp.tanh(warmth)[None, :])
    first_partner = jnp.take(amounts, colliding_pair[:, 0], axis=0)
    second_partner = jnp.take(amounts, colliding_pair[:, 1], axis=0)
    progress = rate_constant * first_partner * second_partner
    gained = jnp.dot(gain_table, progress, precision=lax.Precision.HIGHEST, preferred_element_type=jnp.float32)
    partners = jnp.concatenate([rate_constant * second_partner, rate_constant * first_partner], 0)
    destroyed = jnp.dot(loss_table, partners, precision=lax.Precision.HIGHEST, preferred_element_type=jnp.float32)
    updated = (amounts + step_sizes[None, :] * gained) / (1.0 + step_sizes[None, :] * destroyed)
    warmer = warmth + jnp.dot(formation_warming, updated - amounts, precision=lax.Precision.HIGHEST, preferred_element_type=jnp.float32)
    return jnp.concatenate([updated, warmer[None, :]], 0)


def substep_loop(combined_state_array, counts, turn_count, mechanism):
    step_sizes = chemistry_span / counts.astype(jnp.float32)

    def advance(substep, current):
        advanced = substep_once(current, step_sizes, mechanism)
        return jnp.where((substep < counts)[None, :], advanced, current)

    return lax.fori_loop(0, turn_count, advance, combined_state_array)


def periodic(values):
    return jnp.pad(values, ((0, 0), (3, 3), (3, 3)), mode="wrap")


def reference(component_density, scaled_thermal_state, leading_direction_flow, trailing_direction_flow, spreading_coefficient, colliding_pair, natural_exponent_scaler, arrhenius_energy, stoichiometric_output, formation_warming, explicit_increments):
    combined_state_array = jnp.concatenate([component_density, scaled_thermal_state[None]], 0)
    speed_wide = periodic(jnp.stack([leading_direction_flow, trailing_direction_flow]))
    section_one = combined_state_array + transport_step * tendency(periodic(combined_state_array), speed_wide, spreading_coefficient)
    section_two = 0.75 * combined_state_array + 0.25 * (section_one + transport_step * tendency(periodic(section_one), speed_wide, spreading_coefficient))
    advected = combined_state_array / 3.0 + (2.0 / 3.0) * (section_two + transport_step * tendency(periodic(section_two), speed_wide, spreading_coefficient))
    clipped = jnp.concatenate([jnp.maximum(advected[:-1], 0.0), advected[-1:]], 0)
    layers = SPEC + 1
    blocks = clipped.reshape(layers, N_GX, CX, N_GRP, CY).transpose(3, 1, 0, 2, 4).reshape(N_GRP * N_GX, layers, CX * CY)
    cell_counts = jnp.repeat(explicit_increments.reshape(N_GRP * N_GX, -1), TILE, axis=1)
    gain_table, loss_table = build_tables(colliding_pair, stoichiometric_output)
    mechanism = (gain_table, loss_table, colliding_pair, natural_exponent_scaler, arrhenius_energy, formation_warming)

    def per_device(device_pair):
        device_block, device_counts = device_pair
        return substep_loop(device_block, device_counts, MAXSUB, mechanism)

    reacted = lax.map(per_device, (blocks, cell_counts))
    restored = reacted.reshape(N_GRP, N_GX, layers, CX, CY).transpose(2, 1, 3, 0, 4).reshape(layers, GRID_LENGTH_LEAD, GRID_LENGTH_TRAIL)
    return restored[:SPEC], restored[SPEC]
```

```python
import math

import jax
import jax.numpy as jnp
from jax import lax
from jax.experimental import pallas as pl
from jax.experimental.pallas import tpu as pltpu
from jax.sharding import PartitionSpec as P

SPECIES = 53
ROWS = 56
FT = ROWS // 8
CX, CY = 32, 256
TILES = 64
HALO = 9
WIDE = 384
RXN = 336
GROUP = 8
CELLS = GROUP * 128
DT = 0.4
SPAN = 0.5
FIRST = (0.75, -0.15, 1.0 / 60.0)
SECOND = (1.5, -0.15, 1.0 / 90.0)
CENTER = -49.0 / 18.0
FLOOR = 1e-20
F32, BF16 = jnp.float32, jnp.bfloat16


def two_parts(value):
    high = value.astype(BF16).astype(F32)
    return high, value - high


def pack_kernel(density, thermal, lead, trail, own, first, last, edges):
    for b in range(CX // 8):
        for half in range(2):
            for f in range(ROWS):
                source = density if f < SPECIES else (thermal, lead, trail)[f - SPECIES]
                at = (slice(b * 8, b * 8 + 8), slice(half * 128, half * 128 + 128))
                value = source[(f, *at)] if f < SPECIES else source[at]
                row = (b * 8 * 14 + 2 * (f // 8) + half) * 8 + f % 8
                own[pl.ds(row, 8, stride=14 * 8), :] = value
    lane = lax.broadcasted_iota(jnp.int32, (8, 128), 1)

    def at_row(x, _):
        packed = jnp.zeros((8, 128), F32)
        for t in range(FT):
            row = pl.multiple_of((x * 14 + 2 * t) * 8, 8)
            left = pltpu.roll(own[pl.ds(row, 8), :], 9 * t, 1)
            right = pltpu.roll(own[pl.ds(row + 8, 8), :], (63 + 9 * t - 119) % 128, 1)
            packed = jnp.where((lane >= 9 * t) & (lane < 9 * t + 9), left, packed)
            packed = jnp.where((lane >= 63 + 9 * t) & (lane < 72 + 9 * t), right, packed)
        edges[x] = packed
        return 0

    lax.fori_loop(0, CX, at_row, 0, unroll=2)
    first[...] = own[: HALO * 112, :]
    last[...] = own[(CX - HALO) * 112 :, :]


def run_stage(src, base, base_at, diffusion, speeds, speed_at, rows, block, mix, store):
    keep, take = mix

    def at_block(b, _):
        x0 = b * block
        for t in range(FT):
            r = jnp.concatenate([diffusion[t]] * 3, axis=1)
            rk = [(DT * c) * r for c in SECOND]
            rc = (2.0 * DT * CENTER) * r
            f = [src[x0 + i, t] for i in range(block + 6)]
            q = [speeds[0, speed_at + x0 + i] * f[i] for i in range(block + 6)]
            for i in range(block):
                j = i + 3
                v = speeds[1, speed_at + x0 + j] * f[j]
                total, cross = rc * f[j], None
                for k in (1, 2, 3):
                    total = total + rk[k - 1] * (f[j + k] + f[j - k])
                    total = total - FIRST[k - 1] * (q[j + k] - q[j - k])
                    even = rk[k - 1] * f[j]
                    odd = FIRST[k - 1] * v
                    turned = pltpu.roll(even - odd, WIDE - k, 1) + pltpu.roll(even + odd, k, 1)
                    cross = turned if cross is None else cross + turned
                out = f[j] + (total + cross)
                if keep is not None:
                    out = keep * base[base_at + x0 + i, t] + take * out
                store(x0 + i, t, out)
        return 0

    lax.fori_loop(0, rows // block, at_block, 0)


def react_group(g, counts, order, tiles, gathers, sums, warming, done):
    ids = [order[g * GROUP + i] for i in range(GROUP)]
    number = jnp.concatenate([jnp.full((1, 128), counts[i], jnp.int32) for i in ids], axis=1)
    h = SPAN / number.astype(F32)
    row = lax.broadcasted_iota(jnp.int32, (ROWS, CELLS), 0)
    species = row < SPECIES
    state = jnp.concatenate([tiles[i].reshape(ROWS, 128) for i in ids], axis=1)
    state = jnp.where(species, jnp.maximum(state, 0.0), state)

    def tail(value, a, b, c):
        a = jnp.where(row == SPECIES, a, jnp.where(row == SPECIES + 1, b, c))
        return jnp.where(species, value, a)

    def advance(s, state):
        w = state[SPECIES : SPECIES + 1]
        safe = jnp.maximum(state, FLOOR)
        high, rest = two_parts(jnp.log2(safe))
        middle, low = two_parts(rest)
        heat = jnp.tanh(w)
        heat_0, rest = two_parts(heat)
        heat_1, heat_2 = two_parts(rest)
        stacked = jnp.concatenate(
            [
                tail(high, heat_0, heat_1, 1.0),
                tail(middle, heat_0, 1.0, 1.0),
                tail(low, heat_1, heat_2, heat_0),
            ],
            axis=0,
        ).astype(BF16)
        p = jnp.exp2(jnp.dot(gathers[...], stacked, preferred_element_type=F32))
        high, low = two_parts(p)
        both = jnp.concatenate([high, low], axis=0).astype(BF16)
        totals = jnp.dot(sums[...], both, preferred_element_type=F32)
        gained = totals[:ROWS] + totals[ROWS : 2 * ROWS]
        lost = totals[2 * ROWS : 3 * ROWS]
        updated = safe * (state + h * gained) / (safe + h * lost)
        warm = jnp.concatenate([warming[...]] * GROUP, axis=1)
        rise = jnp.where(species, warm * (updated - state), 0.0)
        warmer = w + jnp.sum(rise, axis=0, keepdims=True)
        after = jnp.where(species, updated, jnp.broadcast_to(warmer, (ROWS, CELLS)))
        return jnp.where(s < number, after, state)

    turns = counts[ids[-1]]
    state = lax.fori_loop(0, turns, advance, state)
    for i in range(GROUP):
        place = (ids[i] & 1) * CX + (ids[i] >> 1)
        at = pl.multiple_of(place * ROWS, 8)
        done[pl.ds(at, ROWS), :] = state[:, i * 128 : i * 128 + 128]


def step_kernel(
    counts,
    order,
    above,
    own,
    below,
    edges_above,
    edges,
    edges_below,
    diffusion,
    gathers,
    sums,
    warming,
    species_out,
    warmth_out,
    slab,
    speeds,
    one,
    two,
    tiles,
    done,
):
    lane = lax.broadcasted_iota(jnp.int32, (8, 128), 1)

    def gather_rows(start, source, sides):
        def at_row(x, _):
            packed = sides[x]
            for t in range(FT):
                after = pltpu.roll(packed, (128 - 9 * t) % 128, 1)
                before = pltpu.roll(packed, (119 - 63 - 9 * t) % 128, 1)
                tile = jnp.where(lane < HALO, after, jnp.where(lane >= 128 - HALO, before, 0.0))
                value = jnp.concatenate([source[x, 2 * t], source[x, 2 * t + 1], tile], axis=1)
                slab[start + x, t] = value
                if t == FT - 1:
                    speeds[0, start + x] = jnp.broadcast_to(DT * value[6:7], (8, WIDE))
                    speeds[1, start + x] = jnp.broadcast_to(DT * value[7:8], (8, WIDE))
            return 0

        lax.fori_loop(0, source.shape[0], at_row, 0)

    gather_rows(0, above, edges_above)
    gather_rows(HALO, own, edges)
    gather_rows(HALO + CX, below, edges_below)

    def to_one(x, t, value):
        one[x, t] = value

    def to_two(x, t, value):
        two[x, t] = value

    def to_tiles(x, t, value):
        tiles[2 * x, t] = value[:, :128]
        tiles[2 * x + 1, t] = value[:, 128:256]

    run_stage(slab, None, 0, diffusion, speeds, 0, 44, 4, (None, None), to_one)
    run_stage(one, slab, 6, diffusion, speeds, 3, 40, 4, (0.75, 0.25), to_two)
    run_stage(two, slab, 9, diffusion, speeds, 6, 32, 4, (1.0 / 3.0, 2.0 / 3.0), to_tiles)

    def at_group(g, _):
        react_group(g, counts, order, tiles, gathers, sums, warming, done)
        return 0

    lax.fori_loop(0, TILES // GROUP, at_group, 0)

    for b in range(CX // 8):
        at = slice(b * 8, b * 8 + 8)
        for half in range(2):
            lanes = slice(half * 128, half * 128 + 128)
            row = (half * CX + b * 8) * ROWS
            for s in range(SPECIES):
                species_out[s, at, lanes] = done[pl.ds(row + s, 8, stride=ROWS), :]
            warmth_out[at, lanes] = done[pl.ds(row + SPECIES, 8, stride=ROWS), :]


def parts(value, number):
    out = []
    for _ in range(number):
        out.append(lax.reduce_precision(value, 8, 7))
        value = value - out[-1]
    return out


def tables(pairs, exponents, energies, output, diffusion, warming):
    extra = RXN - pairs.shape[0]
    padded = jnp.pad(pairs, ((0, extra), (0, 0)), constant_values=-1)
    ids = jnp.arange(SPECIES, dtype=jnp.int32)
    taken = (padded[:, :1] == ids).astype(F32) + (padded[:, 1:] == ids).astype(F32)
    scale = 1.0 / math.log(2.0)
    a = parts(jnp.pad(scale * exponents, (0, extra)), 3)
    e = parts(jnp.pad(scale * energies, (0, extra)), 3)
    tails = [(e[0], e[0], a[0]), (e[1], a[1], a[2]), (e[1], e[0], e[2])]
    gathers = jnp.concatenate([v for tail in tails for v in (taken, jnp.stack(tail, 1))], 1)
    high, low = parts(jnp.pad(output, ((0, extra), (0, ROWS - SPECIES))).T, 2)
    lost = jnp.pad(taken, ((0, 0), (0, ROWS - SPECIES))).T
    sums = jnp.concatenate([high, low, lost, jnp.zeros((8, RXN), F32)], 0)
    sums = jnp.concatenate([sums, sums], 1)

    def column(values):
        values = jnp.pad(values, (0, ROWS - values.shape[0]))
        return jnp.broadcast_to(values[:, None], (ROWS, 128))

    return (column(diffusion).reshape(FT, 8, 128), gathers.astype(BF16), sums.astype(BF16), column(warming))


def ranked(counts):
    number = jnp.arange(TILES, dtype=jnp.int32)
    key = counts * TILES + number
    rank = jnp.sum((key[None, :] < key[:, None]).astype(jnp.int32), axis=1)
    return jnp.sum(jnp.where(rank[None, :] == number[:, None], number[None, :], 0), axis=1)


def neighbours(axis):
    n = lax.axis_size(axis)
    up = [(i, (i + 1) % n) for i in range(n)]
    return up, [(j, i) for i, j in up]


VMEM = pl.BlockSpec(memory_space=pltpu.VMEM)
SMEM = pl.BlockSpec(memory_space=pltpu.SMEM)


def body(density, thermal, lead, trail, diffusion, pairs, exponents, energies, output, warming, counts):
    own, first, last, edges = pl.pallas_call(
        pack_kernel,
        out_shape=(
            jax.ShapeDtypeStruct((CX * 112, 128), F32),
            jax.ShapeDtypeStruct((HALO * 112, 128), F32),
            jax.ShapeDtypeStruct((HALO * 112, 128), F32),
            jax.ShapeDtypeStruct((CX, 8, 128), F32),
        ),
        in_specs=[VMEM] * 4,
        out_specs=(VMEM,) * 4,
        compiler_params=pltpu.CompilerParams(vmem_limit_bytes=16 * 2**20),
        name="pack",
    )(density, thermal, lead, trail)
    up, down = neighbours("grp")
    before = lax.ppermute(edges, "grp", up)
    after = lax.ppermute(edges, "grp", down)
    up, down = neighbours("gx")
    above = lax.ppermute(last, "gx", up)
    below = lax.ppermute(first, "gx", down)
    lane = jnp.arange(128, dtype=jnp.int32)
    sides = jnp.where(lane < 63, after, before)
    sides_above = lax.ppermute(sides[CX - HALO :], "gx", up)
    sides_below = lax.ppermute(sides[:HALO], "gx", down)
    consts = tables(pairs, exponents, energies, output, diffusion, warming)
    return pl.pallas_call(
        step_kernel,
        out_shape=(
            jax.ShapeDtypeStruct((SPECIES, CX, CY), F32),
            jax.ShapeDtypeStruct((CX, CY), F32),
        ),
        in_specs=[SMEM] * 2 + [VMEM] * 10,
        out_specs=(VMEM, VMEM),
        scratch_shapes=[
            pltpu.VMEM((CX + 18, FT, 8, WIDE), F32),
            pltpu.VMEM((2, CX + 18, 8, WIDE), F32),
            pltpu.VMEM((46, FT, 8, WIDE), F32),
            pltpu.VMEM((40, FT, 8, WIDE), F32),
            pltpu.VMEM((TILES, FT, 8, 128), F32),
            pltpu.VMEM((TILES * ROWS, 128), F32),
        ],
        compiler_params=pltpu.CompilerParams(vmem_limit_bytes=50 * 2**20),
        name="transport_and_chemistry",
    )(
        counts,
        ranked(counts),
        above.reshape(HALO, 14, 8, 128),
        own.reshape(CX, 14, 8, 128),
        below.reshape(HALO, 14, 8, 128),
        sides_above,
        sides,
        sides_below,
        *consts,
    )


def solution(mesh):
    return jax.shard_map(
        body,
        mesh=mesh,
        in_specs=(
            P(None, "gx", "grp"),
            P("gx", "grp"),
            P("gx", "grp"),
            P("gx", "grp"),
            P(),
            P(),
            P(),
            P(),
            P(),
            P(),
            P(("grp", "gx")),
        ),
        out_specs=(P(None, "gx", "grp"), P("gx", "grp")),
        check_vma=False,
    )
```

```python
import math

import jax
import jax.numpy as jnp
from jax import lax
from jax.experimental import pallas as pl
from jax.experimental.pallas import tpu as pltpu
from jax.sharding import PartitionSpec as P

SPECIES = 53
ROWS = 56
FT = ROWS // 8
CX, CY = 32, 256
TILES = 64
HALO = 9
WIDE = 384
RXN = 336
GROUP = 8
CELLS = GROUP * 128
DT = 0.4
SPAN = 0.5
FIRST = (0.75, -0.15, 1.0 / 60.0)
SECOND = (1.5, -0.15, 1.0 / 90.0)
CENTER = -49.0 / 18.0
FLOOR = 1e-20
F32, BF16 = jnp.float32, jnp.bfloat16


def two_parts(value):
    high = value.astype(BF16).astype(F32)
    return high, value - high


def pack_kernel(density_hbm, thermal_hbm, lead_hbm, trail_hbm, own, first, last, edges, density, others, sems):
    copies = [pltpu.make_async_copy(density_hbm, density, sems.at[0])]
    for i, source in enumerate((thermal_hbm, lead_hbm, trail_hbm)):
        copies.append(pltpu.make_async_copy(source, others.at[i], sems.at[1 + i]))
    for copy in copies:
        copy.start()
    for copy in copies:
        copy.wait()
    for b in range(CX // 8):
        for half in range(2):
            for f in range(ROWS):
                source, i = (density, f) if f < SPECIES else (others, f - SPECIES)
                value = source[i, b * 8 : b * 8 + 8, half * 128 : half * 128 + 128]
                row = (b * 8 * 14 + 2 * (f // 8) + half) * 8 + f % 8
                own[pl.ds(row, 8, stride=14 * 8), :] = value
    lane = lax.broadcasted_iota(jnp.int32, (8, 128), 1)

    def at_row(x, _):
        packed = jnp.zeros((8, 128), F32)
        for t in range(FT):
            row = pl.multiple_of((x * 14 + 2 * t) * 8, 8)
            left = pltpu.roll(own[pl.ds(row, 8), :], 9 * t, 1)
            right = pltpu.roll(own[pl.ds(row + 8, 8), :], (63 + 9 * t - 119) % 128, 1)
            packed = jnp.where((lane >= 9 * t) & (lane < 9 * t + 9), left, packed)
            packed = jnp.where((lane >= 63 + 9 * t) & (lane < 72 + 9 * t), right, packed)
        edges[x] = packed
        return 0

    lax.fori_loop(0, CX, at_row, 0, unroll=4)
    first[...] = own[: HALO * 112, :]
    last[...] = own[(CX - HALO) * 112 :, :]


def run_stage(src, base, base_at, diffusion, speeds, speed_at, rows, block, mix, store):
    keep, take = mix

    def at_block(b, _):
        x0 = b * block
        for t in range(FT):
            r = jnp.concatenate([diffusion[t]] * 3, axis=1)
            rk = [(DT * c) * r for c in SECOND]
            rc = (2.0 * DT * CENTER) * r
            f = [src[x0 + i, t] for i in range(block + 6)]
            q = [speeds[0, speed_at + x0 + i] * f[i] for i in range(block + 6)]
            for i in range(block):
                j = i + 3
                v = speeds[1, speed_at + x0 + j] * f[j]
                total, cross = rc * f[j], None
                for k in (1, 2, 3):
                    total = total + rk[k - 1] * (f[j + k] + f[j - k])
                    total = total - FIRST[k - 1] * (q[j + k] - q[j - k])
                    even = rk[k - 1] * f[j]
                    odd = FIRST[k - 1] * v
                    turned = pltpu.roll(even - odd, WIDE - k, 1) + pltpu.roll(even + odd, k, 1)
                    cross = turned if cross is None else cross + turned
                out = f[j] + (total + cross)
                if keep is not None:
                    out = keep * base[base_at + x0 + i, t] + take * out
                store(x0 + i, t, out)
        return 0

    lax.fori_loop(0, rows // block, at_block, 0)


def react_group(g, counts, order, tiles, gathers, sums, warming, done):
    ids = [order[g * GROUP + i] for i in range(GROUP)]
    number = jnp.concatenate([jnp.full((1, 128), counts[i], jnp.int32) for i in ids], axis=1)
    h = SPAN / number.astype(F32)
    row = lax.broadcasted_iota(jnp.int32, (ROWS, CELLS), 0)
    species = row < SPECIES
    state = jnp.concatenate([tiles[i].reshape(ROWS, 128) for i in ids], axis=1)
    state = jnp.where(species, jnp.maximum(state, 0.0), state)

    def tail(value, a, b, c):
        a = jnp.where(row == SPECIES, a, jnp.where(row == SPECIES + 1, b, c))
        return jnp.where(species, value, a)

    def advance(s, state):
        w = state[SPECIES : SPECIES + 1]
        safe = jnp.maximum(state, FLOOR)
        high, rest = two_parts(jnp.log2(safe))
        middle, low = two_parts(rest)
        heat = jnp.tanh(w)
        heat_0, rest = two_parts(heat)
        heat_1, heat_2 = two_parts(rest)
        stacked = jnp.concatenate(
            [
                tail(high, heat_0, heat_1, 1.0),
                tail(middle, heat_0, 1.0, 1.0),
                tail(low, heat_1, heat_2, heat_0),
            ],
            axis=0,
        ).astype(BF16)
        p = jnp.exp2(jnp.dot(gathers[...], stacked, preferred_element_type=F32))
        high, low = two_parts(p)
        both = jnp.concatenate([high, low], axis=0).astype(BF16)
        totals = jnp.dot(sums[...], both, preferred_element_type=F32)
        gained = totals[:ROWS] + totals[ROWS : 2 * ROWS]
        lost = totals[2 * ROWS : 3 * ROWS]
        updated = safe * (state + h * gained) / (safe + h * lost)
        warm = jnp.concatenate([warming[...]] * GROUP, axis=1)
        rise = jnp.where(species, warm * (updated - state), 0.0)
        warmer = w + jnp.sum(rise, axis=0, keepdims=True)
        after = jnp.where(species, updated, jnp.broadcast_to(warmer, (ROWS, CELLS)))
        return jnp.where(s < number, after, state)

    turns = counts[ids[-1]]
    state = lax.fori_loop(0, turns, advance, state)
    for i in range(GROUP):
        place = (ids[i] & 1) * CX + (ids[i] >> 1)
        at = pl.multiple_of(place * ROWS, 8)
        done[pl.ds(at, ROWS), :] = state[:, i * 128 : i * 128 + 128]


def step_kernel(
    counts,
    order,
    above,
    own,
    below,
    edges_above,
    edges,
    edges_below,
    diffusion,
    gathers,
    sums,
    warming,
    species_out,
    warmth_out,
    slab,
    speeds,
    one,
    two,
    tiles,
    done,
):
    lane = lax.broadcasted_iota(jnp.int32, (8, 128), 1)

    def gather_rows(start, source, sides):
        def at_row(x, _):
            packed = sides[x]
            for t in range(FT):
                after = pltpu.roll(packed, (128 - 9 * t) % 128, 1)
                before = pltpu.roll(packed, (119 - 63 - 9 * t) % 128, 1)
                tile = jnp.where(lane < HALO, after, jnp.where(lane >= 128 - HALO, before, 0.0))
                value = jnp.concatenate([source[x, 2 * t], source[x, 2 * t + 1], tile], axis=1)
                slab[start + x, t] = value
                if t == FT - 1:
                    speeds[0, start + x] = jnp.broadcast_to(DT * value[6:7], (8, WIDE))
                    speeds[1, start + x] = jnp.broadcast_to(DT * value[7:8], (8, WIDE))
            return 0

        lax.fori_loop(0, source.shape[0], at_row, 0)

    gather_rows(0, above, edges_above)
    gather_rows(HALO, own, edges)
    gather_rows(HALO + CX, below, edges_below)

    def to_one(x, t, value):
        one[x, t] = value

    def to_two(x, t, value):
        two[x, t] = value

    def to_tiles(x, t, value):
        tiles[2 * x, t] = value[:, :128]
        tiles[2 * x + 1, t] = value[:, 128:256]

    run_stage(slab, None, 0, diffusion, speeds, 0, 44, 4, (None, None), to_one)
    run_stage(one, slab, 6, diffusion, speeds, 3, 40, 4, (0.75, 0.25), to_two)
    run_stage(two, slab, 9, diffusion, speeds, 6, 32, 4, (1.0 / 3.0, 2.0 / 3.0), to_tiles)

    def at_group(g, _):
        react_group(g, counts, order, tiles, gathers, sums, warming, done)
        return 0

    lax.fori_loop(0, TILES // GROUP, at_group, 0)

    for b in range(CX // 8):
        at = slice(b * 8, b * 8 + 8)
        for half in range(2):
            lanes = slice(half * 128, half * 128 + 128)
            row = (half * CX + b * 8) * ROWS
            for s in range(SPECIES):
                species_out[s, at, lanes] = done[pl.ds(row + s, 8, stride=ROWS), :]
            warmth_out[at, lanes] = done[pl.ds(row + SPECIES, 8, stride=ROWS), :]


def parts(value, number):
    out = []
    for _ in range(number):
        out.append(lax.reduce_precision(value, 8, 7))
        value = value - out[-1]
    return out


def tables(pairs, exponents, energies, output, diffusion, warming):
    extra = RXN - pairs.shape[0]
    padded = jnp.pad(pairs, ((0, extra), (0, 0)), constant_values=-1).T
    row = jnp.arange(3 * ROWS, dtype=jnp.int32)[:, None]
    ids = row % ROWS
    taken = (padded[:1] == ids).astype(F32) + (padded[1:] == ids).astype(F32)
    scale = 1.0 / math.log(2.0)
    a = parts(jnp.pad(scale * exponents, (0, extra)), 3)
    e = parts(jnp.pad(scale * energies, (0, extra)), 3)
    gathers = taken
    for i, tail in enumerate(((e[0], e[0], a[0]), (e[1], a[1], a[2]), (e[1], e[0], e[2]))):
        for j, value in enumerate(tail):
            gathers = jnp.where(row == i * ROWS + SPECIES + j, value[None], gathers)
    gathers = gathers.T
    high, low = parts(jnp.pad(output, ((0, extra), (0, ROWS - SPECIES))).T, 2)
    sums = jnp.concatenate([high, low, taken[:ROWS], jnp.zeros((8, RXN), F32)], 0)
    sums = jnp.concatenate([sums, sums], 1)

    def column(values):
        values = jnp.pad(values, (0, ROWS - values.shape[0]))
        return jnp.broadcast_to(values[:, None], (ROWS, 128))

    return (column(diffusion).reshape(FT, 8, 128), gathers.astype(BF16), sums.astype(BF16), column(warming))


def ranked(counts):
    number = jnp.arange(TILES, dtype=jnp.int32)
    key = counts * TILES + number
    rank = jnp.sum((key[None, :] < key[:, None]).astype(jnp.int32), axis=1)
    return jnp.sum(jnp.where(rank[None, :] == number[:, None], number[None, :], 0), axis=1)


def neighbours(axis):
    n = lax.axis_size(axis)
    up = [(i, (i + 1) % n) for i in range(n)]
    return up, [(j, i) for i, j in up]


VMEM = pl.BlockSpec(memory_space=pltpu.VMEM)
SMEM = pl.BlockSpec(memory_space=pltpu.SMEM)


def body(density, thermal, lead, trail, diffusion, pairs, exponents, energies, output, warming, counts):
    own, first, last, edges = pl.pallas_call(
        pack_kernel,
        out_shape=(
            jax.ShapeDtypeStruct((CX * 112, 128), F32),
            jax.ShapeDtypeStruct((HALO * 112, 128), F32),
            jax.ShapeDtypeStruct((HALO * 112, 128), F32),
            jax.ShapeDtypeStruct((CX, 8, 128), F32),
        ),
        in_specs=[pl.BlockSpec(memory_space=pl.ANY)] * 4,
        out_specs=(VMEM,) * 4,
        scratch_shapes=[
            pltpu.VMEM((SPECIES, CX, CY), F32),
            pltpu.VMEM((3, CX, CY), F32),
            pltpu.SemaphoreType.DMA((4,)),
        ],
        compiler_params=pltpu.CompilerParams(vmem_limit_bytes=56 * 2**20),
        name="pack",
    )(density, thermal, lead, trail)
    up, down = neighbours("grp")
    before = lax.ppermute(edges, "grp", up)
    after = lax.ppermute(edges, "grp", down)
    up, down = neighbours("gx")
    above = lax.ppermute(last, "gx", up)
    below = lax.ppermute(first, "gx", down)
    lane = jnp.arange(128, dtype=jnp.int32)
    sides = jnp.where(lane < 63, after, before)
    sides_above = lax.ppermute(sides[CX - HALO :], "gx", up)
    sides_below = lax.ppermute(sides[:HALO], "gx", down)
    consts = tables(pairs, exponents, energies, output, diffusion, warming)
    return pl.pallas_call(
        step_kernel,
        out_shape=(
            jax.ShapeDtypeStruct((SPECIES, CX, CY), F32),
            jax.ShapeDtypeStruct((CX, CY), F32),
        ),
        in_specs=[SMEM] * 2 + [VMEM] * 10,
        out_specs=(VMEM, VMEM),
        scratch_shapes=[
            pltpu.VMEM((CX + 18, FT, 8, WIDE), F32),
            pltpu.VMEM((2, CX + 18, 8, WIDE), F32),
            pltpu.VMEM((46, FT, 8, WIDE), F32),
            pltpu.VMEM((40, FT, 8, WIDE), F32),
            pltpu.VMEM((TILES, FT, 8, 128), F32),
            pltpu.VMEM((TILES * ROWS, 128), F32),
        ],
        compiler_params=pltpu.CompilerParams(vmem_limit_bytes=50 * 2**20),
        name="transport_and_chemistry",
    )(
        counts,
        ranked(counts),
        above.reshape(HALO, 14, 8, 128),
        own.reshape(CX, 14, 8, 128),
        below.reshape(HALO, 14, 8, 128),
        sides_above,
        sides,
        sides_below,
        *consts,
    )


def solution(mesh):
    return jax.shard_map(
        body,
        mesh=mesh,
        in_specs=(
            P(None, "gx", "grp"),
            P("gx", "grp"),
            P("gx", "grp"),
            P("gx", "grp"),
            P(),
            P(),
            P(),
            P(),
            P(),
            P(),
            P(("grp", "gx")),
        ),
        out_specs=(P(None, "gx", "grp"), P("gx", "grp")),
        check_vma=False,
    )
```

```python
import math

import jax
import jax.numpy as jnp
from jax import lax
from jax.experimental import pallas as pl
from jax.experimental.pallas import tpu as pltpu
from jax.sharding import PartitionSpec as P

SPECIES = 53
ROWS = 56
FT = ROWS // 8
CX, CY = 32, 256
TILES = 64
HALO = 9
WIDE = 384
RXN = 336
GROUP = 8
CELLS = GROUP * 128
DT = 0.4
SPAN = 0.5
FIRST = (0.75, -0.15, 1.0 / 60.0)
SECOND = (1.5, -0.15, 1.0 / 90.0)
CENTER = -49.0 / 18.0
FLOOR = 1e-20
F32, BF16 = jnp.float32, jnp.bfloat16


def two_parts(value):
    high = value.astype(BF16).astype(F32)
    return high, value - high


def pack_kernel(
    density_hbm,
    thermal_hbm,
    lead_hbm,
    trail_hbm,
    own_hbm,
    first,
    last,
    edges_hbm,
    density,
    others,
    own,
    edges,
    sems,
    out_sems,
):
    copies = []
    for b in range(CX // 8):
        at = slice(b * 8, b * 8 + 8)
        now = [pltpu.make_async_copy(density_hbm.at[:, at], density.at[:, at], sems.at[b, 0])]
        for i, source in enumerate((thermal_hbm, lead_hbm, trail_hbm)):
            now.append(pltpu.make_async_copy(source.at[at], others.at[i, at], sems.at[b, 1 + i]))
        copies.append(now)
    for now in copies:
        for copy in now:
            copy.start()
    lane = lax.broadcasted_iota(jnp.int32, (8, 128), 1)
    for b in range(CX // 8):
        for copy in copies[b]:
            copy.wait()
        for half in range(2):
            for f in range(ROWS):
                source, i = (density, f) if f < SPECIES else (others, f - SPECIES)
                value = source[i, b * 8 : b * 8 + 8, half * 128 : half * 128 + 128]
                row = (b * 8 * 14 + 2 * (f // 8) + half) * 8 + f % 8
                own[pl.ds(row, 8, stride=14 * 8), :] = value
        for x in range(b * 8, b * 8 + 8):
            packed = jnp.zeros((8, 128), F32)
            for t in range(FT):
                row = (x * 14 + 2 * t) * 8
                left = pltpu.roll(own[row : row + 8, :], 9 * t, 1)
                right = pltpu.roll(own[row + 8 : row + 16, :], (63 + 9 * t - 119) % 128, 1)
                packed = jnp.where((lane >= 9 * t) & (lane < 9 * t + 9), left, packed)
                packed = jnp.where((lane >= 63 + 9 * t) & (lane < 72 + 9 * t), right, packed)
            edges[x] = packed
    ends = []
    rows = own.reshape(CX, 14, 8, 128)
    for i, (source, target) in enumerate(
        (
            (edges, edges_hbm),
            (rows.at[:HALO], first.at[:, :14]),
            (rows.at[CX - HALO :], last.at[:, :14]),
            (rows, own_hbm),
        )
    ):
        ends.append(pltpu.make_async_copy(source, target, out_sems.at[i]))
        ends[-1].start()
    for copy in ends:
        copy.wait()


def run_stage(src, base, base_at, diffusion, speeds, speed_at, starts, rows, block, mix, store):
    keep, take = mix

    def at_block(b, _):
        for t, start in ((t, start) for t in range(FT) for start in starts):
            x0 = start + b * block
            r = jnp.concatenate([diffusion[t]] * 3, axis=1)
            rk = [(DT * c) * r for c in SECOND]
            rc = (2.0 * DT * CENTER) * r
            f = [src[x0 + i, t] for i in range(block + 6)]
            q = [speeds[0, speed_at + x0 + i] * f[i] for i in range(block + 6)]
            for i in range(block):
                j = i + 3
                v = speeds[1, speed_at + x0 + j] * f[j]
                total, cross = rc * f[j], None
                for k in (1, 2, 3):
                    total = total + rk[k - 1] * (f[j + k] + f[j - k])
                    total = total - FIRST[k - 1] * (q[j + k] - q[j - k])
                    even = rk[k - 1] * f[j]
                    odd = FIRST[k - 1] * v
                    turned = pltpu.roll(even - odd, WIDE - k, 1) + pltpu.roll(even + odd, k, 1)
                    cross = turned if cross is None else cross + turned
                out = f[j] + (total + cross)
                if keep is not None:
                    out = keep * base[base_at + x0 + i, t] + take * out
                store(x0 + i, t, out)
        return 0

    lax.fori_loop(0, rows // block, at_block, 0)


def react_group(g, counts, order, tiles, gathers, sums, warming, done):
    ids = [order[g * GROUP + i] for i in range(GROUP)]
    number = jnp.concatenate([jnp.full((1, 128), counts[i], jnp.int32) for i in ids], axis=1)
    h = SPAN / number.astype(F32)
    row = lax.broadcasted_iota(jnp.int32, (ROWS, CELLS), 0)
    species = row < SPECIES
    state = jnp.concatenate([tiles[i].reshape(ROWS, 128) for i in ids], axis=1)
    state = jnp.where(species, jnp.maximum(state, 0.0), state)

    def tail(value, a, b, c):
        a = jnp.where(row == SPECIES, a, jnp.where(row == SPECIES + 1, b, c))
        return jnp.where(species, value, a)

    def advance(s, state):
        w = state[SPECIES : SPECIES + 1]
        safe = jnp.maximum(state, FLOOR)
        high, rest = two_parts(jnp.log2(safe))
        middle, low = two_parts(rest)
        heat = jnp.tanh(w)
        heat_0, rest = two_parts(heat)
        heat_1, heat_2 = two_parts(rest)
        stacked = jnp.concatenate(
            [
                tail(high, heat_0, heat_1, 1.0),
                tail(middle, heat_0, 1.0, 1.0),
                tail(low, heat_1, heat_2, heat_0),
            ],
            axis=0,
        ).astype(BF16)
        p = jnp.exp2(jnp.dot(gathers[...], stacked, preferred_element_type=F32))
        high, low = two_parts(p)
        both = jnp.concatenate([high, low], axis=0).astype(BF16)
        totals = jnp.dot(sums[...], both, preferred_element_type=F32)
        gained = totals[:ROWS] + totals[ROWS : 2 * ROWS]
        lost = totals[2 * ROWS : 3 * ROWS]
        updated = safe * (state + h * gained) / (safe + h * lost)
        warm = jnp.concatenate([warming[...]] * GROUP, axis=1)
        rise = jnp.where(species, warm * (updated - state), 0.0)
        warmer = w + jnp.sum(rise, axis=0, keepdims=True)
        after = jnp.where(species, updated, jnp.broadcast_to(warmer, (ROWS, CELLS)))
        return jnp.where(s < number, after, state)

    turns = counts[ids[-1]]
    state = lax.fori_loop(0, turns, advance, state)
    for i in range(GROUP):
        place = (ids[i] & 1) * CX + (ids[i] >> 1)
        at = pl.multiple_of(place * ROWS, 8)
        done[pl.ds(at, ROWS), :] = state[:, i * 128 : i * 128 + 128]


def widen(slab, speeds, at, tiles_of, after, before):
    lane = lax.broadcasted_iota(jnp.int32, (8, 128), 1)
    for t in range(FT):
        right = pltpu.roll(after, (128 - 9 * t) % 128, 1)
        left = pltpu.roll(before, (119 - 63 - 9 * t) % 128, 1)
        tile = jnp.where(lane < HALO, right, jnp.where(lane >= 128 - HALO, left, 0.0))
        value = jnp.concatenate([tiles_of(2 * t), tiles_of(2 * t + 1), tile], axis=1)
        slab[at, t] = value
        if t == FT - 1:
            speeds[0, at] = jnp.broadcast_to(DT * value[6:7], (8, WIDE))
            speeds[1, at] = jnp.broadcast_to(DT * value[7:8], (8, WIDE))


def put(target, shift=0):
    def store(x, t, value):
        target[x + shift, t] = value

    return store


def put_tiles(target, shift=0):
    def store(x, t, value):
        target[2 * (x + shift), t] = value[:, :128]
        target[2 * (x + shift) + 1, t] = value[:, 128:256]

    return store


SECOND_MIX, THIRD_MIX = (0.75, 0.25), (1.0 / 3.0, 2.0 / 3.0)


def inner_kernel(own, before, after, diffusion, one_out, two_out, tiles, slab, speeds, one, two):
    def at_row(x, _):
        widen(slab, speeds, x, lambda j: own[x, j], after[x], before[x])
        return 0

    lax.fori_loop(0, CX, at_row, 0)
    run_stage(slab, None, 0, diffusion, speeds, 0, (0,), 26, 2, (None, None), put(one))
    run_stage(one, slab, 6, diffusion, speeds, 3, (0,), 20, 4, SECOND_MIX, put(two))
    run_stage(two, slab, 9, diffusion, speeds, 6, (0,), 14, 2, THIRD_MIX, put_tiles(tiles))
    for i in range(6):
        one_out[i] = one[i]
        one_out[6 + i] = one[20 + i]
        two_out[i] = two[i]
        two_out[6 + i] = two[14 + i]


def outer_kernel(
    counts,
    order,
    above,
    own,
    before,
    after,
    below,
    one_in,
    two_in,
    tiles_in,
    diffusion,
    gathers,
    sums,
    warming,
    species_out,
    warmth_out,
    slab,
    speeds,
    one,
    two,
    tiles,
    done,
):
    def at_row(x, _):
        widen(slab, speeds, x, lambda j: above[x, j], above[x, 14], above[x, 14])
        widen(slab, speeds, HALO + CX + x, lambda j: below[x, j], below[x, 14], below[x, 14])
        return 0

    def at_own_row(x, _):
        y = CX - 12 + x
        widen(slab, speeds, HALO + x, lambda j: own[x, j], after[x], before[x])
        widen(slab, speeds, HALO + y, lambda j: own[y, j], after[y], before[y])
        return 0

    lax.fori_loop(0, HALO, at_row, 0)
    lax.fori_loop(0, 12, at_own_row, 0)
    for i in range(6):
        one[9 + i] = one_in[i]
        one[29 + i] = one_in[6 + i]
        two[9 + i] = two_in[i]
        two[23 + i] = two_in[6 + i]
    tiles[18:46] = tiles_in[...]
    run_stage(slab, None, 0, diffusion, speeds, 0, (0, 35), 9, 3, (None, None), put(one))
    run_stage(one, slab, 6, diffusion, speeds, 3, (0, 29), 9, 3, SECOND_MIX, put(two))
    run_stage(two, slab, 9, diffusion, speeds, 6, (0, 23), 9, 3, THIRD_MIX, put_tiles(tiles))

    def at_group(g, _):
        react_group(g, counts, order, tiles, gathers, sums, warming, done)
        return 0

    lax.fori_loop(0, TILES // GROUP, at_group, 0)

    for b in range(CX // 8):
        at = slice(b * 8, b * 8 + 8)
        for half in range(2):
            lanes = slice(half * 128, half * 128 + 128)
            row = (half * CX + b * 8) * ROWS
            for s in range(SPECIES):
                species_out[s, at, lanes] = done[pl.ds(row + s, 8, stride=ROWS), :]
            warmth_out[at, lanes] = done[pl.ds(row + SPECIES, 8, stride=ROWS), :]


def parts(value, number):
    out = []
    for _ in range(number):
        out.append(lax.reduce_precision(value, 8, 7))
        value = value - out[-1]
    return out


def tables(pairs, exponents, energies, output, diffusion, warming):
    extra = RXN - pairs.shape[0]
    padded = jnp.pad(pairs, ((0, extra), (0, 0)), constant_values=-1).T
    row = jnp.arange(3 * ROWS, dtype=jnp.int32)[:, None]
    ids = row % ROWS
    taken = (padded[:1] == ids).astype(F32) + (padded[1:] == ids).astype(F32)
    scale = 1.0 / math.log(2.0)
    a = parts(jnp.pad(scale * exponents, (0, extra)), 3)
    e = parts(jnp.pad(scale * energies, (0, extra)), 3)
    gathers = taken
    for i, tail in enumerate(((e[0], e[0], a[0]), (e[1], a[1], a[2]), (e[1], e[0], e[2]))):
        for j, value in enumerate(tail):
            gathers = jnp.where(row == i * ROWS + SPECIES + j, value[None], gathers)
    gathers = gathers.T
    high, low = parts(jnp.pad(output, ((0, extra), (0, ROWS - SPECIES))).T, 2)
    sums = jnp.concatenate([high, low, taken[:ROWS], jnp.zeros((8, RXN), F32)], 0)
    sums = jnp.concatenate([sums, sums], 1)

    def column(values):
        values = jnp.pad(values, (0, ROWS - values.shape[0]))
        return jnp.broadcast_to(values[:, None], (ROWS, 128))

    return (column(diffusion).reshape(FT, 8, 128), gathers.astype(BF16), sums.astype(BF16), column(warming))


def ranked(counts):
    number = jnp.arange(TILES, dtype=jnp.int32)
    key = counts * TILES + number
    rank = jnp.sum((key[None, :] < key[:, None]).astype(jnp.int32), axis=1)
    return jnp.sum(jnp.where(rank[None, :] == number[:, None], number[None, :], 0), axis=1)


def neighbours(axis):
    n = lax.axis_size(axis)
    up = [(i, (i + 1) % n) for i in range(n)]
    return up, [(j, i) for i, j in up]


VMEM = pl.BlockSpec(memory_space=pltpu.VMEM)
SMEM = pl.BlockSpec(memory_space=pltpu.SMEM)


def body(density, thermal, lead, trail, diffusion, pairs, exponents, energies, output, warming, counts):
    own, first, last, edges = pl.pallas_call(
        pack_kernel,
        out_shape=(
            jax.ShapeDtypeStruct((CX, 14, 8, 128), F32),
            jax.ShapeDtypeStruct((HALO, 15, 8, 128), F32),
            jax.ShapeDtypeStruct((HALO, 15, 8, 128), F32),
            jax.ShapeDtypeStruct((CX, 8, 128), F32),
        ),
        in_specs=[pl.BlockSpec(memory_space=pltpu.HBM)] * 4,
        out_specs=(pl.BlockSpec(memory_space=pltpu.HBM),) * 4,
        scratch_shapes=[
            pltpu.VMEM((SPECIES, CX, CY), F32),
            pltpu.VMEM((3, CX, CY), F32),
            pltpu.VMEM((CX * 112, 128), F32),
            pltpu.VMEM((CX, 8, 128), F32),
            pltpu.SemaphoreType.DMA((CX // 8, 4)),
            pltpu.SemaphoreType.DMA((4,)),
        ],
        compiler_params=pltpu.CompilerParams(vmem_limit_bytes=55 * 2**20),
        name="pack",
    )(density, thermal, lead, trail)
    up, down = neighbours("grp")
    before = lax.ppermute(edges, "grp", up)
    after = lax.ppermute(edges, "grp", down)
    side = jnp.arange(128, dtype=jnp.int32) < 63
    first = first.at[:, 14].set(jnp.where(side, after[:HALO], before[:HALO]))
    last = last.at[:, 14].set(jnp.where(side, after[CX - HALO :], before[CX - HALO :]))
    up, down = neighbours("gx")
    above = lax.ppermute(last, "gx", up)
    below = lax.ppermute(first, "gx", down)
    spread, gathers, sums, warm = tables(pairs, exponents, energies, output, diffusion, warming)
    one, two, tiles = pl.pallas_call(
        inner_kernel,
        out_shape=(
            jax.ShapeDtypeStruct((12, FT, 8, WIDE), F32),
            jax.ShapeDtypeStruct((12, FT, 8, WIDE), F32),
            jax.ShapeDtypeStruct((28, FT, 8, 128), F32),
        ),
        in_specs=[VMEM] * 4,
        out_specs=(VMEM,) * 3,
        scratch_shapes=[
            pltpu.VMEM((CX, FT, 8, WIDE), F32),
            pltpu.VMEM((2, CX, 8, WIDE), F32),
            pltpu.VMEM((26, FT, 8, WIDE), F32),
            pltpu.VMEM((20, FT, 8, WIDE), F32),
        ],
        compiler_params=pltpu.CompilerParams(vmem_limit_bytes=20 * 2**20),
        cost_estimate=pl.CostEstimate(flops=10**9, bytes_accessed=30 * 10**6, transcendentals=0),
        name="inner_transport",
    )(own, before, after, spread)
    return pl.pallas_call(
        outer_kernel,
        out_shape=(
            jax.ShapeDtypeStruct((SPECIES, CX, CY), F32),
            jax.ShapeDtypeStruct((CX, CY), F32),
        ),
        in_specs=[SMEM] * 2 + [VMEM] * 12,
        out_specs=(VMEM, VMEM),
        scratch_shapes=[
            pltpu.VMEM((CX + 18, FT, 8, WIDE), F32),
            pltpu.VMEM((2, CX + 18, 8, WIDE), F32),
            pltpu.VMEM((44, FT, 8, WIDE), F32),
            pltpu.VMEM((38, FT, 8, WIDE), F32),
            pltpu.VMEM((TILES, FT, 8, 128), F32),
            pltpu.VMEM((TILES * ROWS, 128), F32),
        ],
        compiler_params=pltpu.CompilerParams(vmem_limit_bytes=36 * 2**20),
        name="outer_transport_and_chemistry",
    )(counts, ranked(counts), above, own, before, after, below, one, two, tiles, spread, gathers, sums, warm)


def solution(mesh):
    return jax.shard_map(
        body,
        mesh=mesh,
        in_specs=(
            P(None, "gx", "grp"),
            P("gx", "grp"),
            P("gx", "grp"),
            P("gx", "grp"),
            P(),
            P(),
            P(),
            P(),
            P(),
            P(),
            P(("grp", "gx")),
        ),
        out_specs=(P(None, "gx", "grp"), P("gx", "grp")),
        check_vma=False,
    )
```

```python
import functools
import math

import jax
import jax.numpy as jnp
from jax import lax
from jax.experimental import pallas as pl
from jax.experimental.pallas import tpu as pltpu
from jax.sharding import PartitionSpec as P

SPECIES = 53
ROWS = 56
FT = ROWS // 8
CX, CY = 32, 256
TILES = 64
HALO = 9
WIDE = 384
RXN = 336
GROUP = 8
CELLS = GROUP * 128
DT = 0.4
SPAN = 0.5
FIRST = (0.75, -0.15, 1.0 / 60.0)
CENTER = -49.0 / 18.0
FLOOR = 1e-20
F32, BF16 = jnp.float32, jnp.bfloat16


def two_parts(value):
    high = value.astype(BF16).astype(F32)
    return high, value - high


def pack_kernel(
    density_hbm,
    thermal_hbm,
    lead_hbm,
    trail_hbm,
    own_hbm,
    first,
    last,
    left_hbm,
    right_hbm,
    density,
    others,
    own,
    left_edges,
    right_edges,
    sems,
    out_sems,
):
    copies = []
    for b in range(CX // 8):
        at = slice(b * 8, b * 8 + 8)
        now = [pltpu.make_async_copy(density_hbm.at[:, at], density.at[:, at], sems.at[b, 0])]
        for i, source in enumerate((thermal_hbm, lead_hbm, trail_hbm)):
            now.append(pltpu.make_async_copy(source.at[at], others.at[i, at], sems.at[b, 1 + i]))
        copies.append(now)
    for now in copies:
        for copy in now:
            copy.start()
    lane = lax.broadcasted_iota(jnp.int32, (8, 128), 1)
    for b in range(CX // 8):
        for copy in copies[b]:
            copy.wait()
        for half in range(2):
            for f in range(ROWS):
                source, i = (density, f) if f < SPECIES else (others, f - SPECIES)
                value = source[i, b * 8 : b * 8 + 8, half * 128 : half * 128 + 128]
                row = (b * 8 * 14 + 2 * (f // 8) + half) * 8 + f % 8
                own[pl.ds(row, 8, stride=14 * 8), :] = value
    for x in range(CX // 2):
        sides = []
        for edge, places in ((0, (0, 63)), (119, (63, 0))):
            packed = jnp.zeros((8, 128), F32)
            for y, place in zip((x, x + CX // 2), places):
                for t in range(FT):
                    row = (y * 14 + 2 * t + (edge > 0)) * 8
                    at = place + 9 * t
                    turned = pltpu.roll(own[row : row + 8, :], (at - edge) % 128, 1)
                    packed = jnp.where((lane >= at) & (lane < at + HALO), turned, packed)
            sides.append(packed)
        left_edges[x], right_edges[x] = sides
    ends = []
    rows = own.reshape(CX, 14, 8, 128)
    for i, (source, target) in enumerate(
        (
            (left_edges, left_hbm),
            (right_edges, right_hbm),
            (rows.at[:HALO], first.at[:, :14]),
            (rows.at[CX - HALO :], last.at[:, :14]),
            (rows, own_hbm),
        )
    ):
        ends.append(pltpu.make_async_copy(source, target, out_sems.at[i]))
        ends[-1].start()
    for copy in ends:
        copy.wait()


def stage_block(b, src, base, base_at, diffusion, speeds, speed_at, starts, block, mix, store):
    keep, take = mix
    for t, start in ((t, start) for t in range(FT) for start in starts):
        x0 = start + b * block
        r = jnp.concatenate([diffusion[t]] * 3, axis=1)
        pull = [(2.0 / k) * r for k in (1, 2, 3)]
        rc = (2.0 * DT * CENTER) * r
        f = [src[x0 + i, t] for i in range(block + 6)]
        q = [speeds[0, speed_at + x0 + i] * f[i] for i in range(block + 6)]
        for i in range(block):
            j = i + 3
            v = speeds[1, speed_at + x0 + j] * f[j]
            total = rc * f[j]
            for k in (1, 2, 3):
                even = pull[k - 1] * f[j]
                turned = pltpu.roll(even - v, WIDE - k, 1) + pltpu.roll(even + v, k, 1)
                along = pull[k - 1] * (f[j + k] + f[j - k]) - (q[j + k] - q[j - k])
                total = total + (DT * FIRST[k - 1]) * (turned + along)
            out = f[j] + total
            if keep is not None:
                out = keep * base[base_at + x0 + i, t] + take * out
            store(x0 + i, t, out)


def run_stage(src, base, base_at, diffusion, speeds, speed_at, starts, rows, block, mix, store):
    def at_block(b, _):
        stage_block(b, src, base, base_at, diffusion, speeds, speed_at, starts, block, mix, store)
        return 0

    lax.fori_loop(0, rows // block, at_block, 0)


def react_group(g, counts, order, tiles, gathers, sums, warming, done, beside=()):
    ids = [order[g * GROUP + i] for i in range(GROUP)]
    per_tile = [counts[i] for i in ids]
    number = jnp.concatenate([jnp.full((1, 128), n, jnp.int32) for n in per_tile], axis=1)
    h = SPAN / number.astype(F32)
    row = lax.broadcasted_iota(jnp.int32, (ROWS, CELLS), 0)
    species = row < SPECIES
    state = jnp.concatenate([tiles[i].reshape(ROWS, 128) for i in ids], axis=1)
    state = jnp.where(species, jnp.maximum(state, 0.0), state)

    def tail(value, a, b, c):
        a = jnp.where(row == SPECIES, a, jnp.where(row == SPECIES + 1, b, c))
        return jnp.where(species, value, a)

    def advance(s, state):
        w = state[SPECIES : SPECIES + 1]
        safe = jnp.maximum(state, FLOOR)
        high, rest = two_parts(jnp.log2(safe))
        middle, low = two_parts(rest)
        heat = jnp.tanh(w)
        heat_0, rest = two_parts(heat)
        heat_1, heat_2 = two_parts(rest)
        stacked = jnp.concatenate(
            [
                tail(high, heat_0, heat_1, 1.0),
                tail(middle, heat_0, 1.0, 1.0),
                tail(low, heat_1, heat_2, heat_0),
            ],
            axis=0,
        ).astype(BF16)
        p = jnp.exp2(jnp.dot(gathers[...], stacked, preferred_element_type=F32))
        high, low = two_parts(p)
        both = jnp.concatenate([high, low], axis=0).astype(BF16)
        totals = jnp.dot(sums[...], both, preferred_element_type=F32)
        gained = totals[:ROWS] + totals[ROWS : 2 * ROWS]
        lost = totals[2 * ROWS : 3 * ROWS]
        updated = safe * (state + h * gained) / (safe + h * lost)
        warm = jnp.concatenate([warming[...]] * GROUP, axis=1)
        rise = jnp.where(species, warm * (updated - state), 0.0)
        warmer = w + jnp.sum(rise, axis=0, keepdims=True)
        after = jnp.where(species, updated, jnp.broadcast_to(warmer, (ROWS, CELLS)))
        return jnp.where(s < number, after, state)

    turns = functools.reduce(jnp.maximum, per_tile)
    if beside:
        turns_beside, work = beside

        def both(s, state):
            work(s)
            return advance(s, state)

        state = lax.fori_loop(0, turns_beside, both, state)
        state = lax.fori_loop(turns_beside, turns, advance, state)
    else:
        state = lax.fori_loop(0, turns, advance, state)
    for i in range(GROUP):
        place = (ids[i] & 1) * CX + (ids[i] >> 1)
        at = pl.multiple_of(place * ROWS, 8)
        done[pl.ds(at, ROWS), :] = state[:, i * 128 : i * 128 + 128]


def widen(slab, speeds, at, tiles_of, after, before, after_at, before_at):
    lane = lax.broadcasted_iota(jnp.int32, (8, 128), 1)
    for t in range(FT):
        right = pltpu.roll(after, (-after_at - 9 * t) % 128, 1)
        left = pltpu.roll(before, (119 - before_at - 9 * t) % 128, 1)
        tile = jnp.where(lane < HALO, right, jnp.where(lane >= 128 - HALO, left, 0.0))
        value = jnp.concatenate([tiles_of(2 * t), tiles_of(2 * t + 1), tile], axis=1)
        slab[at, t] = value
        if t == FT - 1:
            speeds[0, at] = jnp.broadcast_to(value[6:7], (8, WIDE))
            speeds[1, at] = jnp.broadcast_to(value[7:8], (8, WIDE))


def put(target, shift=0):
    def store(x, t, value):
        target[x + shift, t] = value

    return store


def put_tiles(target, shift=0):
    def store(x, t, value):
        target[2 * (x + shift), t] = value[:, :128]
        target[2 * (x + shift) + 1, t] = value[:, 128:256]

    return store


SECOND_MIX, THIRD_MIX = (0.75, 0.25), (1.0 / 3.0, 2.0 / 3.0)


def inner_kernel(own, before, after, diffusion, one_out, two_out, tiles, slab, speeds, one, two):
    def at_row(x, _):
        y = x + CX // 2
        widen(slab, speeds, x, lambda j: own[x, j], after[x], before[x], 0, 63)
        widen(slab, speeds, y, lambda j: own[y, j], after[x], before[x], 63, 0)
        return 0

    lax.fori_loop(0, CX // 2, at_row, 0, unroll=2)
    run_stage(slab, None, 0, diffusion, speeds, 0, (0,), 26, 2, (None, None), put(one))
    run_stage(one, slab, 6, diffusion, speeds, 3, (0,), 20, 4, SECOND_MIX, put(two))
    run_stage(two, slab, 9, diffusion, speeds, 6, (0,), 14, 2, THIRD_MIX, put_tiles(tiles))
    for i in range(6):
        one_out[i] = one[i]
        one_out[6 + i] = one[20 + i]
        two_out[i] = two[i]
        two_out[6 + i] = two[14 + i]


def outer_kernel(
    counts,
    order,
    above,
    own,
    before,
    after,
    below,
    one_in,
    two_in,
    tiles_in,
    diffusion,
    gathers,
    sums,
    warming,
    species_hbm,
    warmth_hbm,
    slab,
    speeds,
    one,
    two,
    tiles,
    done,
    species_out,
    warmth_out,
    sems,
):
    def at_row(x, _):
        widen(slab, speeds, x, lambda j: above[x, j], above[x, 14], above[x, 14], 63, 0)
        widen(slab, speeds, HALO + CX + x, lambda j: below[x, j], below[x, 14], below[x, 14], 0, 63)
        return 0

    def at_own_row(x, _):
        y, z = CX - 12 + x, CX // 2 - 12 + x
        widen(slab, speeds, HALO + x, lambda j: own[x, j], after[x], before[x], 0, 63)
        widen(slab, speeds, HALO + y, lambda j: own[y, j], after[z], before[z], 63, 0)
        return 0

    lax.fori_loop(0, HALO, at_row, 0, unroll=3)
    lax.fori_loop(0, 12, at_own_row, 0, unroll=2)
    for i in range(6):
        one[9 + i] = one_in[i]
        one[29 + i] = one_in[6 + i]
        two[9 + i] = two_in[i]
        two[23 + i] = two_in[6 + i]
    tiles[18:46] = tiles_in[...]
    args = (diffusion, speeds)
    stages = (
        (slab, None, 0, *args, 0, (0, 35), 3, (None, None), put(one)),
        (one, slab, 6, *args, 3, (0, 29), 3, SECOND_MIX, put(two)),
        (two, slab, 9, *args, 6, (0, 23), 3, THIRD_MIX, put_tiles(tiles)),
    )
    mechanism = (counts, order, tiles, gathers, sums, warming, done)
    for g, stage in enumerate(stages):
        react_group(g, *mechanism, beside=(3, lambda b: stage_block(b, *stage)))

    def at_group(g, _):
        react_group(g, *mechanism)
        return 0

    lax.fori_loop(3, TILES // GROUP, at_group, 0)

    copies = []
    for b in range(CX // 8):
        at = slice(b * 8, b * 8 + 8)
        for half in range(2):
            lanes = slice(half * 128, half * 128 + 128)
            row = (half * CX + b * 8) * ROWS
            for s in range(SPECIES):
                species_out[s, at, lanes] = done[pl.ds(row + s, 8, stride=ROWS), :]
            warmth_out[at, lanes] = done[pl.ds(row + SPECIES, 8, stride=ROWS), :]
        copies.append(pltpu.make_async_copy(species_out.at[:, at], species_hbm.at[:, at], sems.at[b]))
        copies[-1].start()
    copies.append(pltpu.make_async_copy(warmth_out, warmth_hbm, sems.at[CX // 8]))
    copies[-1].start()
    for copy in copies:
        copy.wait()


def parts(value, number):
    out = []
    for _ in range(number):
        out.append(lax.reduce_precision(value, 8, 7))
        value = value - out[-1]
    return out


def tables(pairs, exponents, energies, output, diffusion, warming):
    extra = RXN - pairs.shape[0]
    padded = jnp.pad(pairs, ((0, extra), (0, 0)), constant_values=-1).T
    row = jnp.arange(3 * ROWS, dtype=jnp.int32)[:, None]
    ids = row % ROWS
    taken = (padded[:1] == ids).astype(F32) + (padded[1:] == ids).astype(F32)
    scale = 1.0 / math.log(2.0)
    a = parts(jnp.pad(scale * exponents, (0, extra)), 3)
    e = parts(jnp.pad(scale * energies, (0, extra)), 3)
    gathers = taken
    for i, tail in enumerate(((e[0], e[0], a[0]), (e[1], a[1], a[2]), (e[1], e[0], e[2]))):
        for j, value in enumerate(tail):
            gathers = jnp.where(row == i * ROWS + SPECIES + j, value[None], gathers)
    gathers = gathers.T
    high, low = parts(jnp.pad(output, ((0, extra), (0, ROWS - SPECIES))).T, 2)
    sums = jnp.concatenate([high, low, taken[:ROWS], jnp.zeros((8, RXN), F32)], 0)
    sums = jnp.concatenate([sums, sums], 1)

    def column(values):
        values = jnp.pad(values, (0, ROWS - values.shape[0]))
        return jnp.broadcast_to(values[:, None], (ROWS, 128))

    return (column(diffusion).reshape(FT, 8, 128), gathers.astype(BF16), sums.astype(BF16), column(warming))


def ranked(counts):
    number = jnp.arange(TILES, dtype=jnp.int32)
    outer = jnp.where((number >= 18) & (number < 46), 0, 8 * TILES)
    key = outer + counts * TILES + number
    rank = jnp.sum((key[None, :] < key[:, None]).astype(jnp.int32), axis=1)
    rank = jnp.where(rank < 28, (rank + 24) % 28, rank)
    return jnp.sum(jnp.where(rank[None, :] == number[:, None], number[None, :], 0), axis=1)


def neighbours(axis):
    n = lax.axis_size(axis)
    up = [(i, (i + 1) % n) for i in range(n)]
    return up, [(j, i) for i, j in up]


VMEM = pl.BlockSpec(memory_space=pltpu.VMEM)
SMEM = pl.BlockSpec(memory_space=pltpu.SMEM)


def body(density, thermal, lead, trail, diffusion, pairs, exponents, energies, output, warming, counts):
    own, first, last, left, right = pl.pallas_call(
        pack_kernel,
        out_shape=(
            jax.ShapeDtypeStruct((CX, 14, 8, 128), F32),
            jax.ShapeDtypeStruct((HALO, 15, 8, 128), F32),
            jax.ShapeDtypeStruct((HALO, 15, 8, 128), F32),
            jax.ShapeDtypeStruct((CX // 2, 8, 128), F32),
            jax.ShapeDtypeStruct((CX // 2, 8, 128), F32),
        ),
        in_specs=[pl.BlockSpec(memory_space=pltpu.HBM)] * 4,
        out_specs=(pl.BlockSpec(memory_space=pltpu.HBM),) * 5,
        scratch_shapes=[
            pltpu.VMEM((SPECIES, CX, CY), F32),
            pltpu.VMEM((3, CX, CY), F32),
            pltpu.VMEM((CX * 112, 128), F32),
            pltpu.VMEM((CX // 2, 8, 128), F32),
            pltpu.VMEM((CX // 2, 8, 128), F32),
            pltpu.SemaphoreType.DMA((CX // 8, 4)),
            pltpu.SemaphoreType.DMA((5,)),
        ],
        compiler_params=pltpu.CompilerParams(vmem_limit_bytes=55 * 2**20),
        name="pack",
    )(density, thermal, lead, trail)
    up, down = neighbours("grp")
    before = lax.ppermute(right, "grp", up)
    after = lax.ppermute(left, "grp", down)
    side = jnp.arange(128, dtype=jnp.int32) < 63
    first = first.at[:, 14].set(jnp.where(side, after[:HALO], before[:HALO]))
    last = last.at[:, 14].set(jnp.where(side, before[-HALO:], after[-HALO:]))
    up, down = neighbours("gx")
    above = lax.ppermute(last, "gx", up)
    below = lax.ppermute(first, "gx", down)
    spread, gathers, sums, warm = tables(pairs, exponents, energies, output, diffusion, warming)
    one, two, tiles = pl.pallas_call(
        inner_kernel,
        out_shape=(
            jax.ShapeDtypeStruct((12, FT, 8, WIDE), F32),
            jax.ShapeDtypeStruct((12, FT, 8, WIDE), F32),
            jax.ShapeDtypeStruct((28, FT, 8, 128), F32),
        ),
        in_specs=[VMEM] * 4,
        out_specs=(VMEM,) * 3,
        scratch_shapes=[
            pltpu.VMEM((CX, FT, 8, WIDE), F32),
            pltpu.VMEM((2, CX, 8, WIDE), F32),
            pltpu.VMEM((26, FT, 8, WIDE), F32),
            pltpu.VMEM((20, FT, 8, WIDE), F32),
        ],
        compiler_params=pltpu.CompilerParams(vmem_limit_bytes=20 * 2**20),
        cost_estimate=pl.CostEstimate(flops=10**9, bytes_accessed=30 * 10**6, transcendentals=0),
        name="inner_transport",
    )(own, before, after, spread)
    return pl.pallas_call(
        outer_kernel,
        out_shape=(
            jax.ShapeDtypeStruct((SPECIES, CX, CY), F32),
            jax.ShapeDtypeStruct((CX, CY), F32),
        ),
        in_specs=[SMEM] * 2 + [VMEM] * 12,
        out_specs=(pl.BlockSpec(memory_space=pltpu.HBM),) * 2,
        scratch_shapes=[
            pltpu.VMEM((CX + 18, FT, 8, WIDE), F32),
            pltpu.VMEM((2, CX + 18, 8, WIDE), F32),
            pltpu.VMEM((44, FT, 8, WIDE), F32),
            pltpu.VMEM((38, FT, 8, WIDE), F32),
            pltpu.VMEM((TILES, FT, 8, 128), F32),
            pltpu.VMEM((TILES * ROWS, 128), F32),
            pltpu.VMEM((SPECIES, CX, CY), F32),
            pltpu.VMEM((CX, CY), F32),
            pltpu.SemaphoreType.DMA((CX // 8 + 1,)),
        ],
        compiler_params=pltpu.CompilerParams(vmem_limit_bytes=36 * 2**20),
        name="outer_transport_and_chemistry",
    )(counts, ranked(counts), above, own, before, after, below, one, two, tiles, spread, gathers, sums, warm)


def solution(mesh):
    return jax.shard_map(
        body,
        mesh=mesh,
        in_specs=(
            P(None, "gx", "grp"),
            P("gx", "grp"),
            P("gx", "grp"),
            P("gx", "grp"),
            P(),
            P(),
            P(),
            P(),
            P(),
            P(),
            P(("grp", "gx")),
        ),
        out_specs=(P(None, "gx", "grp"), P("gx", "grp")),
        check_vma=False,
    )
```

```python
import functools
import math

import jax
import jax.numpy as jnp
from jax import lax
from jax.experimental import pallas as pl
from jax.experimental.pallas import tpu as pltpu
from jax.sharding import PartitionSpec as P

SPECIES = 53
ROWS = 56
FT = ROWS // 8
CX, CY = 32, 256
TILES = 64
HALO = 9
WIDE = 384
RXN = 336
GROUP = 8
CELLS = GROUP * 128
DT = 0.4
SPAN = 0.5
FIRST = (0.75, -0.15, 1.0 / 60.0)
CENTER = -49.0 / 18.0
FLOOR = 1e-20
F32, BF16 = jnp.float32, jnp.bfloat16


def two_parts(value):
    high = value.astype(BF16).astype(F32)
    return high, value - high


def pack_kernel(
    density_hbm,
    thermal_hbm,
    lead_hbm,
    trail_hbm,
    own_hbm,
    first,
    last,
    left_hbm,
    right_hbm,
    density,
    others,
    own,
    left_edges,
    right_edges,
    sems,
    out_sems,
):
    copies = []
    for b in range(CX // 8):
        at = slice(b * 8, b * 8 + 8)
        now = [pltpu.make_async_copy(density_hbm.at[:, at], density.at[:, at], sems.at[b, 0])]
        for i, source in enumerate((thermal_hbm, lead_hbm, trail_hbm)):
            now.append(pltpu.make_async_copy(source.at[at], others.at[i, at], sems.at[b, 1 + i]))
        copies.append(now)
    for now in copies:
        for copy in now:
            copy.start()
    lane = lax.broadcasted_iota(jnp.int32, (8, 128), 1)
    for b in range(CX // 8):
        for copy in copies[b]:
            copy.wait()
        for half in range(2):
            for f in range(ROWS):
                source, i = (density, f) if f < SPECIES else (others, f - SPECIES)
                value = source[i, b * 8 : b * 8 + 8, half * 128 : half * 128 + 128]
                row = (b * 8 * 14 + 2 * (f // 8) + half) * 8 + f % 8
                own[pl.ds(row, 8, stride=14 * 8), :] = value
    for x in range(CX // 2):
        sides = []
        for edge, places in ((0, (0, 63)), (119, (63, 0))):
            packed = jnp.zeros((8, 128), F32)
            for y, place in zip((x, x + CX // 2), places):
                for t in range(FT):
                    row = (y * 14 + 2 * t + (edge > 0)) * 8
                    at = place + 9 * t
                    turned = pltpu.roll(own[row : row + 8, :], (at - edge) % 128, 1)
                    packed = jnp.where((lane >= at) & (lane < at + HALO), turned, packed)
            sides.append(packed)
        left_edges[x], right_edges[x] = sides
    ends = []
    rows = own.reshape(CX, 14, 8, 128)
    for i, (source, target) in enumerate(
        (
            (left_edges, left_hbm),
            (right_edges, right_hbm),
            (rows.at[:HALO], first.at[:, :14]),
            (rows.at[CX - HALO :], last.at[:, :14]),
            (rows, own_hbm),
        )
    ):
        ends.append(pltpu.make_async_copy(source, target, out_sems.at[i]))
        ends[-1].start()
    for copy in ends:
        copy.wait()


def stage_block(b, src, base, base_at, diffusion, speeds, speed_at, starts, block, mix, store):
    keep, take = mix
    for t, start in ((t, start) for t in range(FT) for start in starts):
        x0 = start + b * block
        r = jnp.concatenate([diffusion[t]] * 3, axis=1)
        pull = [(2.0 / k) * r for k in (1, 2, 3)]
        rc = (2.0 * DT * CENTER) * r
        f = [src[x0 + i, t] for i in range(block + 6)]
        q = [speeds[0, speed_at + x0 + i] * f[i] for i in range(block + 6)]
        for i in range(block):
            j = i + 3
            v = speeds[1, speed_at + x0 + j] * f[j]
            total = rc * f[j]
            for k in (1, 2, 3):
                even = pull[k - 1] * f[j]
                turned = pltpu.roll(even - v, WIDE - k, 1) + pltpu.roll(even + v, k, 1)
                along = pull[k - 1] * (f[j + k] + f[j - k]) - (q[j + k] - q[j - k])
                total = total + (DT * FIRST[k - 1]) * (turned + along)
            out = f[j] + total
            if keep is not None:
                out = keep * base[base_at + x0 + i, t] + take * out
            store(x0 + i, t, out)


def run_stage(src, base, base_at, diffusion, speeds, speed_at, starts, rows, block, mix, store):
    def at_block(b, _):
        stage_block(b, src, base, base_at, diffusion, speeds, speed_at, starts, block, mix, store)
        return 0

    lax.fori_loop(0, rows // block, at_block, 0)


def react_group(g, counts, order, tiles, gathers, sums, warming, done, beside=()):
    ids = [order[g * GROUP + i] for i in range(GROUP)]
    per_tile = [counts[i] for i in ids]
    number = jnp.concatenate([jnp.full((1, 128), n, jnp.int32) for n in per_tile], axis=1)
    h = SPAN / number.astype(F32)
    row = lax.broadcasted_iota(jnp.int32, (ROWS, CELLS), 0)
    species = row < SPECIES
    state = jnp.concatenate([tiles[i].reshape(ROWS, 128) for i in ids], axis=1)
    state = jnp.where(species, jnp.maximum(state, 0.0), state)

    def tail(value, a, b, c):
        a = jnp.where(row == SPECIES, a, jnp.where(row == SPECIES + 1, b, c))
        return jnp.where(species, value, a)

    def advance(s, state):
        w = state[SPECIES : SPECIES + 1]
        safe = jnp.maximum(state, FLOOR)
        high, rest = two_parts(jnp.log2(safe))
        middle, low = two_parts(rest)
        heat = jnp.tanh(w)
        heat_0, rest = two_parts(heat)
        heat_1, heat_2 = two_parts(rest)
        stacked = jnp.concatenate(
            [
                tail(high, heat_0, heat_1, 1.0),
                tail(middle, heat_0, 1.0, 1.0),
                tail(low, heat_1, heat_2, heat_0),
            ],
            axis=0,
        ).astype(BF16)
        p = jnp.exp2(jnp.dot(gathers[...], stacked, preferred_element_type=F32))
        high, low = two_parts(p)
        both = jnp.concatenate([high, low], axis=0).astype(BF16)
        totals = jnp.dot(sums[...], both, preferred_element_type=F32)
        gained = totals[:ROWS] + totals[ROWS : 2 * ROWS]
        lost = totals[2 * ROWS : 3 * ROWS]
        updated = safe * (state + h * gained) / (safe + h * lost)
        warm = jnp.concatenate([warming[...]] * GROUP, axis=1)
        rise = jnp.where(species, warm * (updated - state), 0.0)
        warmer = w + jnp.sum(rise, axis=0, keepdims=True)
        after = jnp.where(species, updated, jnp.broadcast_to(warmer, (ROWS, CELLS)))
        return jnp.where(s < number, after, state)

    turns = functools.reduce(jnp.maximum, per_tile)
    if beside:
        turns_beside, work = beside

        def both(s, state):
            work(s)
            return advance(s, state)

        state = lax.fori_loop(0, turns_beside, both, state)
        state = lax.fori_loop(turns_beside, turns, advance, state)
    else:
        state = lax.fori_loop(0, turns, advance, state)
    for i in range(GROUP):
        place = (ids[i] & 1) * CX + (ids[i] >> 1)
        at = pl.multiple_of(place * ROWS, 8)
        done[pl.ds(at, ROWS), :] = state[:, i * 128 : i * 128 + 128]


def widen(slab, speeds, at, tiles_of, after, before, after_at, before_at):
    lane = lax.broadcasted_iota(jnp.int32, (8, 128), 1)
    for t in range(FT):
        right = pltpu.roll(after, (-after_at - 9 * t) % 128, 1)
        left = pltpu.roll(before, (119 - before_at - 9 * t) % 128, 1)
        tile = jnp.where(lane < HALO, right, jnp.where(lane >= 128 - HALO, left, 0.0))
        value = jnp.concatenate([tiles_of(2 * t), tiles_of(2 * t + 1), tile], axis=1)
        slab[at, t] = value
        if t == FT - 1:
            speeds[0, at] = jnp.broadcast_to(value[6:7], (8, WIDE))
            speeds[1, at] = jnp.broadcast_to(value[7:8], (8, WIDE))


def put(target, shift=0):
    def store(x, t, value):
        target[x + shift, t] = value

    return store


def put_tiles(target, shift=0):
    def store(x, t, value):
        target[2 * (x + shift), t] = value[:, :128]
        target[2 * (x + shift) + 1, t] = value[:, 128:256]

    return store


SECOND_MIX, THIRD_MIX = (0.75, 0.25), (1.0 / 3.0, 2.0 / 3.0)


def inner_kernel(own, before, after, diffusion, one_out, two_out, tiles, slab, speeds, one, two):
    def at_row(x, _):
        y = x + CX // 2
        widen(slab, speeds, x, lambda j: own[x, j], after[x], before[x], 0, 63)
        widen(slab, speeds, y, lambda j: own[y, j], after[x], before[x], 63, 0)
        return 0

    lax.fori_loop(0, CX // 2, at_row, 0, unroll=2)
    run_stage(slab, None, 0, diffusion, speeds, 0, (0,), 26, 2, (None, None), put(one))
    run_stage(one, slab, 6, diffusion, speeds, 3, (0,), 20, 4, SECOND_MIX, put(two))
    run_stage(two, slab, 9, diffusion, speeds, 6, (0,), 14, 2, THIRD_MIX, put_tiles(tiles))
    for i in range(6):
        one_out[i] = one[i]
        one_out[6 + i] = one[20 + i]
        two_out[i] = two[i]
        two_out[6 + i] = two[14 + i]


def outer_kernel(
    counts,
    order,
    above,
    own,
    before,
    after,
    below,
    one_in,
    two_in,
    tiles_in,
    diffusion,
    gathers,
    sums,
    warming,
    species_hbm,
    warmth_hbm,
    slab,
    speeds,
    one,
    two,
    tiles,
    done,
    species_out,
    warmth_out,
    sems,
):
    def at_row(x, _):
        widen(slab, speeds, x, lambda j: above[x, j], above[x, 14], above[x, 14], 63, 0)
        widen(slab, speeds, HALO + CX + x, lambda j: below[x, j], below[x, 14], below[x, 14], 0, 63)
        return 0

    def at_own_row(x, _):
        y, z = CX - 12 + x, CX // 2 - 12 + x
        widen(slab, speeds, HALO + x, lambda j: own[x, j], after[x], before[x], 0, 63)
        widen(slab, speeds, HALO + y, lambda j: own[y, j], after[z], before[z], 63, 0)
        return 0

    lax.fori_loop(0, HALO, at_row, 0, unroll=3)
    lax.fori_loop(0, 12, at_own_row, 0, unroll=2)
    for i in range(6):
        one[9 + i] = one_in[i]
        one[29 + i] = one_in[6 + i]
        two[9 + i] = two_in[i]
        two[23 + i] = two_in[6 + i]
    tiles[18:46] = tiles_in[...]
    args = (diffusion, speeds)
    stages = (
        (slab, None, 0, *args, 0, (0, 35), 3, (None, None), put(one)),
        (one, slab, 6, *args, 3, (0, 29), 3, SECOND_MIX, put(two)),
        (two, slab, 9, *args, 6, (0, 23), 3, THIRD_MIX, put_tiles(tiles)),
    )
    mechanism = (counts, order, tiles, gathers, sums, warming, done)
    for g, stage in enumerate(stages):
        react_group(g, *mechanism, beside=(3, lambda b: stage_block(b, *stage)))

    def at_group(g, _):
        react_group(g, *mechanism)
        return 0

    lax.fori_loop(3, TILES // GROUP, at_group, 0)

    copies = []
    for b in range(CX // 8):
        at = slice(b * 8, b * 8 + 8)
        for half in range(2):
            lanes = slice(half * 128, half * 128 + 128)
            row = (half * CX + b * 8) * ROWS
            for s in range(SPECIES):
                species_out[s, at, lanes] = done[pl.ds(row + s, 8, stride=ROWS), :]
            warmth_out[at, lanes] = done[pl.ds(row + SPECIES, 8, stride=ROWS), :]
        copies.append(pltpu.make_async_copy(species_out.at[:, at], species_hbm.at[:, at], sems.at[b]))
        copies[-1].start()
    copies.append(pltpu.make_async_copy(warmth_out, warmth_hbm, sems.at[CX // 8]))
    copies[-1].start()
    for copy in copies:
        copy.wait()


def parts(value, number):
    out = []
    for _ in range(number):
        out.append(lax.reduce_precision(value, 8, 7))
        value = value - out[-1]
    return out


def fetch_kernel(source, own):
    own[...] = source[...]


def tables(pairs, exponents, energies, output, diffusion, warming):
    extra = RXN - pairs.shape[0]
    padded = jnp.pad(pairs, ((0, extra), (0, 0)), constant_values=-1).T
    row = jnp.arange(3 * ROWS, dtype=jnp.int32)[:, None]
    ids = row % ROWS
    taken = (padded[:1] == ids).astype(F32) + (padded[1:] == ids).astype(F32)
    scale = 1.0 / math.log(2.0)
    a = parts(jnp.pad(scale * exponents, (0, extra)), 3)
    e = parts(jnp.pad(scale * energies, (0, extra)), 3)
    gathers = taken
    for i, tail in enumerate(((e[0], e[0], a[0]), (e[1], a[1], a[2]), (e[1], e[0], e[2]))):
        for j, value in enumerate(tail):
            gathers = jnp.where(row == i * ROWS + SPECIES + j, value[None], gathers)
    gathers = gathers.T
    high, low = parts(jnp.pad(output, ((0, extra), (0, ROWS - SPECIES))).T, 2)
    sums = jnp.concatenate([high, low, taken[:ROWS], jnp.zeros((8, RXN), F32)], 0)
    sums = jnp.concatenate([sums, sums], 1)

    def column(values):
        values = jnp.pad(values, (0, ROWS - values.shape[0]))
        return jnp.broadcast_to(values[:, None], (ROWS, 128))

    return (column(diffusion).reshape(FT, 8, 128), gathers.astype(BF16), sums.astype(BF16), column(warming))


def ranked(counts):
    number = jnp.arange(TILES, dtype=jnp.int32)
    outer = jnp.where((number >= 18) & (number < 46), 0, 8 * TILES)
    key = outer + counts * TILES + number
    rank = jnp.sum((key[None, :] < key[:, None]).astype(jnp.int32), axis=1)
    rank = jnp.where(rank < 28, (rank + 24) % 28, rank)
    return jnp.sum(jnp.where(rank[None, :] == number[:, None], number[None, :], 0), axis=1)


def neighbours(axis):
    n = lax.axis_size(axis)
    up = [(i, (i + 1) % n) for i in range(n)]
    return up, [(j, i) for i, j in up]


VMEM = pl.BlockSpec(memory_space=pltpu.VMEM)
SMEM = pl.BlockSpec(memory_space=pltpu.SMEM)


def body(density, thermal, lead, trail, diffusion, pairs, exponents, energies, output, warming, counts):
    own, first, last, left, right = pl.pallas_call(
        pack_kernel,
        out_shape=(
            jax.ShapeDtypeStruct((CX, 14, 8, 128), F32),
            jax.ShapeDtypeStruct((HALO, 15, 8, 128), F32),
            jax.ShapeDtypeStruct((HALO, 15, 8, 128), F32),
            jax.ShapeDtypeStruct((CX // 2, 8, 128), F32),
            jax.ShapeDtypeStruct((CX // 2, 8, 128), F32),
        ),
        in_specs=[pl.BlockSpec(memory_space=pltpu.HBM)] * 4,
        out_specs=(pl.BlockSpec(memory_space=pltpu.HBM),) * 5,
        scratch_shapes=[
            pltpu.VMEM((SPECIES, CX, CY), F32),
            pltpu.VMEM((3, CX, CY), F32),
            pltpu.VMEM((CX * 112, 128), F32),
            pltpu.VMEM((CX // 2, 8, 128), F32),
            pltpu.VMEM((CX // 2, 8, 128), F32),
            pltpu.SemaphoreType.DMA((CX // 8, 4)),
            pltpu.SemaphoreType.DMA((5,)),
        ],
        compiler_params=pltpu.CompilerParams(vmem_limit_bytes=55 * 2**20),
        name="pack",
    )(density, thermal, lead, trail)
    up, down = neighbours("grp")
    before = lax.ppermute(right, "grp", up)
    after = lax.ppermute(left, "grp", down)
    consts = tables(pairs, exponents, energies, output, diffusion, warming)
    own = pl.pallas_call(
        fetch_kernel,
        out_shape=jax.ShapeDtypeStruct((CX, 14, 8, 128), F32),
        in_specs=[VMEM],
        out_specs=VMEM,
        compiler_params=pltpu.CompilerParams(vmem_limit_bytes=16 * 2**20),
        name="fetch",
    )(own)
    before, after, own, rank, (spread, gathers, sums, warm) = lax.optimization_barrier(
        (before, after, own, ranked(counts), consts)
    )
    side = jnp.arange(128, dtype=jnp.int32) < 63
    first = first.at[:, 14].set(jnp.where(side, after[:HALO], before[:HALO]))
    last = last.at[:, 14].set(jnp.where(side, before[-HALO:], after[-HALO:]))
    up, down = neighbours("gx")
    above = lax.ppermute(last, "gx", up)
    below = lax.ppermute(first, "gx", down)
    one, two, tiles = pl.pallas_call(
        inner_kernel,
        out_shape=(
            jax.ShapeDtypeStruct((12, FT, 8, WIDE), F32),
            jax.ShapeDtypeStruct((12, FT, 8, WIDE), F32),
            jax.ShapeDtypeStruct((28, FT, 8, 128), F32),
        ),
        in_specs=[VMEM] * 4,
        out_specs=(VMEM,) * 3,
        scratch_shapes=[
            pltpu.VMEM((CX, FT, 8, WIDE), F32),
            pltpu.VMEM((2, CX, 8, WIDE), F32),
            pltpu.VMEM((26, FT, 8, WIDE), F32),
            pltpu.VMEM((20, FT, 8, WIDE), F32),
        ],
        compiler_params=pltpu.CompilerParams(vmem_limit_bytes=20 * 2**20),
        cost_estimate=pl.CostEstimate(flops=10**9, bytes_accessed=30 * 10**6, transcendentals=0),
        name="inner_transport",
    )(own, before, after, spread)
    return pl.pallas_call(
        outer_kernel,
        out_shape=(
            jax.ShapeDtypeStruct((SPECIES, CX, CY), F32),
            jax.ShapeDtypeStruct((CX, CY), F32),
        ),
        in_specs=[SMEM] * 2 + [VMEM] * 12,
        out_specs=(pl.BlockSpec(memory_space=pltpu.HBM),) * 2,
        scratch_shapes=[
            pltpu.VMEM((CX + 18, FT, 8, WIDE), F32),
            pltpu.VMEM((2, CX + 18, 8, WIDE), F32),
            pltpu.VMEM((44, FT, 8, WIDE), F32),
            pltpu.VMEM((38, FT, 8, WIDE), F32),
            pltpu.VMEM((TILES, FT, 8, 128), F32),
            pltpu.VMEM((TILES * ROWS, 128), F32),
            pltpu.VMEM((SPECIES, CX, CY), F32),
            pltpu.VMEM((CX, CY), F32),
            pltpu.SemaphoreType.DMA((CX // 8 + 1,)),
        ],
        compiler_params=pltpu.CompilerParams(vmem_limit_bytes=36 * 2**20),
        name="outer_transport_and_chemistry",
    )(counts, rank, above, own, before, after, below, one, two, tiles, spread, gathers, sums, warm)


def solution(mesh):
    return jax.shard_map(
        body,
        mesh=mesh,
        in_specs=(
            P(None, "gx", "grp"),
            P("gx", "grp"),
            P("gx", "grp"),
            P("gx", "grp"),
            P(),
            P(),
            P(),
            P(),
            P(),
            P(),
            P(("grp", "gx")),
        ),
        out_specs=(P(None, "gx", "grp"), P("gx", "grp")),
        check_vma=False,
    )
```

```python
import functools
import math

import jax
import jax.numpy as jnp
from jax import lax
from jax.experimental import pallas as pl
from jax.experimental.pallas import tpu as pltpu
from jax.sharding import PartitionSpec as P

SPECIES = 53
ROWS = 56
FT = ROWS // 8
CX, CY = 32, 256
TILES = 64
HALO = 9
WIDE = 384
RXN = 336
GROUP = 8
CELLS = GROUP * 128
DT = 0.4
SPAN = 0.5
FIRST = (0.75, -0.15, 1.0 / 60.0)
CENTER = -49.0 / 18.0
FLOOR = 1e-20
F32, BF16 = jnp.float32, jnp.bfloat16


def two_parts(value):
    high = value.astype(BF16).astype(F32)
    return high, value - high


def pack_kernel(
    density_hbm,
    thermal_hbm,
    lead_hbm,
    trail_hbm,
    own_hbm,
    first,
    last,
    left_hbm,
    right_hbm,
    density,
    others,
    own,
    left_edges,
    right_edges,
    sems,
    out_sems,
):
    copies = []
    for b in range(CX // 8):
        at = slice(b * 8, b * 8 + 8)
        now = [pltpu.make_async_copy(density_hbm.at[:, at], density.at[:, at], sems.at[b, 0])]
        for i, source in enumerate((thermal_hbm, lead_hbm, trail_hbm)):
            now.append(pltpu.make_async_copy(source.at[at], others.at[i, at], sems.at[b, 1 + i]))
        copies.append(now)
    for now in copies:
        for copy in now:
            copy.start()
    lane = lax.broadcasted_iota(jnp.int32, (8, 128), 1)
    rows = own.reshape(CX, 14, 8, 128)
    ends = []

    def send(source, target):
        ends.append(pltpu.make_async_copy(source, target, out_sems.at[len(ends)]))
        ends[-1].start()

    for b in range(CX // 8):
        for copy in copies[b]:
            copy.wait()
        for half in range(2):
            for f in range(ROWS):
                source, i = (density, f) if f < SPECIES else (others, f - SPECIES)
                value = source[i, b * 8 : b * 8 + 8, half * 128 : half * 128 + 128]
                row = (b * 8 * 14 + 2 * (f // 8) + half) * 8 + f % 8
                own[pl.ds(row, 8, stride=14 * 8), :] = value
        if b == 1:
            send(rows.at[:HALO], first.at[:, :14])
            send(rows.at[: CX // 2], own_hbm.at[: CX // 2])
        if b == 3:
            send(rows.at[CX - HALO :], last.at[:, :14])
            send(rows.at[CX // 2 :], own_hbm.at[CX // 2 :])
    for x in range(CX // 2):
        sides = []
        for edge, places in ((0, (0, 63)), (119, (63, 0))):
            packed = jnp.zeros((8, 128), F32)
            for y, place in zip((x, x + CX // 2), places):
                for t in range(FT):
                    row = (y * 14 + 2 * t + (edge > 0)) * 8
                    at = place + 9 * t
                    turned = pltpu.roll(own[row : row + 8, :], (at - edge) % 128, 1)
                    packed = jnp.where((lane >= at) & (lane < at + HALO), turned, packed)
            sides.append(packed)
        left_edges[x], right_edges[x] = sides
    send(left_edges, left_hbm)
    send(right_edges, right_hbm)
    for copy in ends:
        copy.wait()


def stage_block(b, src, base, base_at, diffusion, speeds, speed_at, starts, block, mix, store):
    keep, take = mix
    for t, start in ((t, start) for t in range(FT) for start in starts):
        x0 = start + b * block
        r = jnp.concatenate([diffusion[t]] * 3, axis=1)
        pull = [(2.0 / k) * r for k in (1, 2, 3)]
        rc = (2.0 * DT * CENTER) * r
        f = [src[x0 + i, t] for i in range(block + 6)]
        q = [speeds[0, speed_at + x0 + i] * f[i] for i in range(block + 6)]
        for i in range(block):
            j = i + 3
            v = speeds[1, speed_at + x0 + j] * f[j]
            total = rc * f[j]
            for k in (1, 2, 3):
                even = pull[k - 1] * f[j]
                turned = pltpu.roll(even - v, WIDE - k, 1) + pltpu.roll(even + v, k, 1)
                along = pull[k - 1] * (f[j + k] + f[j - k]) - (q[j + k] - q[j - k])
                total = total + (DT * FIRST[k - 1]) * (turned + along)
            out = f[j] + total
            if keep is not None:
                out = keep * base[base_at + x0 + i, t] + take * out
            store(x0 + i, t, out)


def run_stage(src, base, base_at, diffusion, speeds, speed_at, starts, rows, block, mix, store):
    def at_block(b, _):
        stage_block(b, src, base, base_at, diffusion, speeds, speed_at, starts, block, mix, store)
        return 0

    lax.fori_loop(0, rows // block, at_block, 0)


def react_group(g, counts, order, tiles, gathers, sums, warming, done, beside=()):
    ids = [order[g * GROUP + i] for i in range(GROUP)]
    per_tile = [counts[i] for i in ids]
    number = jnp.concatenate([jnp.full((1, 128), n, jnp.int32) for n in per_tile], axis=1)
    h = SPAN / number.astype(F32)
    row = lax.broadcasted_iota(jnp.int32, (ROWS, CELLS), 0)
    species = row < SPECIES
    state = jnp.concatenate([tiles[i].reshape(ROWS, 128) for i in ids], axis=1)
    state = jnp.where(species, jnp.maximum(state, 0.0), state)

    def tail(value, a, b, c):
        a = jnp.where(row == SPECIES, a, jnp.where(row == SPECIES + 1, b, c))
        return jnp.where(species, value, a)

    def advance(s, state):
        w = state[SPECIES : SPECIES + 1]
        safe = jnp.maximum(state, FLOOR)
        high, rest = two_parts(jnp.log2(safe))
        middle, low = two_parts(rest)
        heat = jnp.tanh(w)
        heat_0, rest = two_parts(heat)
        heat_1, heat_2 = two_parts(rest)
        stacked = jnp.concatenate(
            [
                tail(high, heat_0, heat_1, 1.0),
                tail(middle, heat_0, 1.0, 1.0),
                tail(low, heat_1, heat_2, heat_0),
            ],
            axis=0,
        ).astype(BF16)
        p = jnp.exp2(jnp.dot(gathers[...], stacked, preferred_element_type=F32))
        high, low = two_parts(p)
        both = jnp.concatenate([high, low], axis=0).astype(BF16)
        totals = jnp.dot(sums[...], both, preferred_element_type=F32)
        gained = totals[:ROWS] + totals[ROWS : 2 * ROWS]
        lost = totals[2 * ROWS : 3 * ROWS]
        updated = safe * (state + h * gained) / (safe + h * lost)
        warm = jnp.concatenate([warming[...]] * GROUP, axis=1)
        rise = jnp.where(species, warm * (updated - state), 0.0)
        warmer = w + jnp.sum(rise, axis=0, keepdims=True)
        after = jnp.where(species, updated, jnp.broadcast_to(warmer, (ROWS, CELLS)))
        return jnp.where(s < number, after, state)

    turns = functools.reduce(jnp.maximum, per_tile)
    if beside:
        turns_beside, work = beside

        def both(s, state):
            work(s)
            return advance(s, state)

        state = lax.fori_loop(0, turns_beside, both, state)
        state = lax.fori_loop(turns_beside, turns, advance, state)
    else:
        state = lax.fori_loop(0, turns, advance, state)
    for i in range(GROUP):
        place = (ids[i] & 1) * CX + (ids[i] >> 1)
        at = pl.multiple_of(place * ROWS, 8)
        done[pl.ds(at, ROWS), :] = state[:, i * 128 : i * 128 + 128]


def widen(slab, speeds, at, tiles_of, after, before, after_at, before_at):
    lane = lax.broadcasted_iota(jnp.int32, (8, 128), 1)
    for t in range(FT):
        right = pltpu.roll(after, (-after_at - 9 * t) % 128, 1)
        left = pltpu.roll(before, (119 - before_at - 9 * t) % 128, 1)
        tile = jnp.where(lane < HALO, right, jnp.where(lane >= 128 - HALO, left, 0.0))
        value = jnp.concatenate([tiles_of(2 * t), tiles_of(2 * t + 1), tile], axis=1)
        slab[at, t] = value
        if t == FT - 1:
            speeds[0, at] = jnp.broadcast_to(value[6:7], (8, WIDE))
            speeds[1, at] = jnp.broadcast_to(value[7:8], (8, WIDE))


def put(target, shift=0):
    def store(x, t, value):
        target[x + shift, t] = value

    return store


def put_tiles(target, shift=0):
    def store(x, t, value):
        target[2 * (x + shift), t] = value[:, :128]
        target[2 * (x + shift) + 1, t] = value[:, 128:256]

    return store


SECOND_MIX, THIRD_MIX = (0.75, 0.25), (1.0 / 3.0, 2.0 / 3.0)


def inner_kernel(own, before, after, diffusion, one_out, two_out, tiles, slab, speeds, one, two):
    def at_row(x, _):
        y = x + CX // 2
        widen(slab, speeds, x, lambda j: own[x, j], after[x], before[x], 0, 63)
        widen(slab, speeds, y, lambda j: own[y, j], after[x], before[x], 63, 0)
        return 0

    lax.fori_loop(0, CX // 2, at_row, 0, unroll=2)
    run_stage(slab, None, 0, diffusion, speeds, 0, (0,), 26, 13, (None, None), put(one))
    run_stage(one, slab, 6, diffusion, speeds, 3, (0,), 20, 10, SECOND_MIX, put(two))
    run_stage(two, slab, 9, diffusion, speeds, 6, (0,), 14, 7, THIRD_MIX, put_tiles(tiles))
    for i in range(6):
        one_out[i] = one[i]
        one_out[6 + i] = one[20 + i]
        two_out[i] = two[i]
        two_out[6 + i] = two[14 + i]


def outer_kernel(
    counts,
    order,
    above,
    own,
    before,
    after,
    below,
    one_in,
    two_in,
    tiles_in,
    diffusion,
    gathers,
    sums,
    warming,
    species_hbm,
    warmth_hbm,
    slab,
    speeds,
    one,
    two,
    tiles,
    done,
    species_out,
    warmth_out,
    sems,
):
    def at_row(x, _):
        widen(slab, speeds, x, lambda j: above[x, j], above[x, 14], above[x, 14], 63, 0)
        widen(slab, speeds, HALO + CX + x, lambda j: below[x, j], below[x, 14], below[x, 14], 0, 63)
        return 0

    def at_own_row(x, _):
        y, z = CX - 12 + x, CX // 2 - 12 + x
        widen(slab, speeds, HALO + x, lambda j: own[x, j], after[x], before[x], 0, 63)
        widen(slab, speeds, HALO + y, lambda j: own[y, j], after[z], before[z], 63, 0)
        return 0

    lax.fori_loop(0, HALO, at_row, 0, unroll=3)
    lax.fori_loop(0, 12, at_own_row, 0, unroll=2)
    for i in range(6):
        one[9 + i] = one_in[i]
        one[29 + i] = one_in[6 + i]
        two[9 + i] = two_in[i]
        two[23 + i] = two_in[6 + i]
    tiles[18:46] = tiles_in[...]
    args = (diffusion, speeds)
    stages = (
        (slab, None, 0, *args, 0, (0, 35), 9, (None, None), put(one)),
        (one, slab, 6, *args, 3, (0, 29), 9, SECOND_MIX, put(two)),
        (two, slab, 9, *args, 6, (0, 23), 9, THIRD_MIX, put_tiles(tiles)),
    )
    mechanism = (counts, order, tiles, gathers, sums, warming, done)
    for g, stage in enumerate(stages):
        react_group(g, *mechanism, beside=(1, lambda b: stage_block(b, *stage)))

    def at_group(g, _):
        react_group(g, *mechanism)
        return 0

    lax.fori_loop(3, TILES // GROUP, at_group, 0)

    copies = []
    for b in range(CX // 8):
        at = slice(b * 8, b * 8 + 8)
        for half in range(2):
            lanes = slice(half * 128, half * 128 + 128)
            row = (half * CX + b * 8) * ROWS
            for s in range(SPECIES):
                species_out[s, at, lanes] = done[pl.ds(row + s, 8, stride=ROWS), :]
            warmth_out[at, lanes] = done[pl.ds(row + SPECIES, 8, stride=ROWS), :]
        copies.append(pltpu.make_async_copy(species_out.at[:, at], species_hbm.at[:, at], sems.at[b]))
        copies[-1].start()
    copies.append(pltpu.make_async_copy(warmth_out, warmth_hbm, sems.at[CX // 8]))
    copies[-1].start()
    for copy in copies:
        copy.wait()


def parts(value, number):
    out = []
    for _ in range(number):
        out.append(lax.reduce_precision(value, 8, 7))
        value = value - out[-1]
    return out


def fetch_kernel(source, own):
    own[...] = source[...]


def tables(pairs, exponents, energies, output, diffusion, warming):
    extra = RXN - pairs.shape[0]
    padded = jnp.pad(pairs, ((0, extra), (0, 0)), constant_values=-1).T
    row = jnp.arange(3 * ROWS, dtype=jnp.int32)[:, None]
    ids = row % ROWS
    taken = (padded[:1] == ids).astype(F32) + (padded[1:] == ids).astype(F32)
    scale = 1.0 / math.log(2.0)
    a = parts(jnp.pad(scale * exponents, (0, extra)), 3)
    e = parts(jnp.pad(scale * energies, (0, extra)), 3)
    gathers = taken
    for i, tail in enumerate(((e[0], e[0], a[0]), (e[1], a[1], a[2]), (e[1], e[0], e[2]))):
        for j, value in enumerate(tail):
            gathers = jnp.where(row == i * ROWS + SPECIES + j, value[None], gathers)
    gathers = gathers.T
    high, low = parts(jnp.pad(output, ((0, extra), (0, ROWS - SPECIES))).T, 2)
    sums = jnp.concatenate([high, low, taken[:ROWS], jnp.zeros((8, RXN), F32)], 0)
    sums = jnp.concatenate([sums, sums], 1)

    def column(values):
        values = jnp.pad(values, (0, ROWS - values.shape[0]))
        return jnp.broadcast_to(values[:, None], (ROWS, 128))

    return (column(diffusion).reshape(FT, 8, 128), gathers.astype(BF16), sums.astype(BF16), column(warming))


def ranked(counts):
    number = jnp.arange(TILES, dtype=jnp.int32)
    outer = jnp.where((number >= 18) & (number < 46), 0, 8 * TILES)
    key = outer + counts * TILES + number
    rank = jnp.sum((key[None, :] < key[:, None]).astype(jnp.int32), axis=1)
    rank = jnp.where(rank < 28, (rank + 24) % 28, rank)
    return jnp.sum(jnp.where(rank[None, :] == number[:, None], number[None, :], 0), axis=1)


def neighbours(axis):
    n = lax.axis_size(axis)
    up = [(i, (i + 1) % n) for i in range(n)]
    return up, [(j, i) for i, j in up]


VMEM = pl.BlockSpec(memory_space=pltpu.VMEM)
SMEM = pl.BlockSpec(memory_space=pltpu.SMEM)


def body(density, thermal, lead, trail, diffusion, pairs, exponents, energies, output, warming, counts):
    own, first, last, left, right = pl.pallas_call(
        pack_kernel,
        out_shape=(
            jax.ShapeDtypeStruct((CX, 14, 8, 128), F32),
            jax.ShapeDtypeStruct((HALO, 15, 8, 128), F32),
            jax.ShapeDtypeStruct((HALO, 15, 8, 128), F32),
            jax.ShapeDtypeStruct((CX // 2, 8, 128), F32),
            jax.ShapeDtypeStruct((CX // 2, 8, 128), F32),
        ),
        in_specs=[pl.BlockSpec(memory_space=pltpu.HBM)] * 4,
        out_specs=(pl.BlockSpec(memory_space=pltpu.HBM),) * 5,
        scratch_shapes=[
            pltpu.VMEM((SPECIES, CX, CY), F32),
            pltpu.VMEM((3, CX, CY), F32),
            pltpu.VMEM((CX * 112, 128), F32),
            pltpu.VMEM((CX // 2, 8, 128), F32),
            pltpu.VMEM((CX // 2, 8, 128), F32),
            pltpu.SemaphoreType.DMA((CX // 8, 4)),
            pltpu.SemaphoreType.DMA((6,)),
        ],
        compiler_params=pltpu.CompilerParams(vmem_limit_bytes=55 * 2**20),
        name="pack",
    )(density, thermal, lead, trail)
    up, down = neighbours("grp")
    before = lax.ppermute(right, "grp", up)
    after = lax.ppermute(left, "grp", down)
    consts = tables(pairs, exponents, energies, output, diffusion, warming)
    own = pl.pallas_call(
        fetch_kernel,
        out_shape=jax.ShapeDtypeStruct((CX, 14, 8, 128), F32),
        in_specs=[VMEM],
        out_specs=VMEM,
        compiler_params=pltpu.CompilerParams(vmem_limit_bytes=16 * 2**20),
        name="fetch",
    )(own)
    before, after, own, rank, (spread, gathers, sums, warm) = lax.optimization_barrier(
        (before, after, own, ranked(counts), consts)
    )
    side = jnp.arange(128, dtype=jnp.int32) < 63
    first = first.at[:, 14].set(jnp.where(side, after[:HALO], before[:HALO]))
    last = last.at[:, 14].set(jnp.where(side, before[-HALO:], after[-HALO:]))
    up, down = neighbours("gx")
    above = lax.ppermute(last, "gx", up)
    below = lax.ppermute(first, "gx", down)
    one, two, tiles = pl.pallas_call(
        inner_kernel,
        out_shape=(
            jax.ShapeDtypeStruct((12, FT, 8, WIDE), F32),
            jax.ShapeDtypeStruct((12, FT, 8, WIDE), F32),
            jax.ShapeDtypeStruct((28, FT, 8, 128), F32),
        ),
        in_specs=[VMEM] * 4,
        out_specs=(VMEM,) * 3,
        scratch_shapes=[
            pltpu.VMEM((CX, FT, 8, WIDE), F32),
            pltpu.VMEM((2, CX, 8, WIDE), F32),
            pltpu.VMEM((26, FT, 8, WIDE), F32),
            pltpu.VMEM((20, FT, 8, WIDE), F32),
        ],
        compiler_params=pltpu.CompilerParams(vmem_limit_bytes=20 * 2**20),
        cost_estimate=pl.CostEstimate(flops=10**9, bytes_accessed=30 * 10**6, transcendentals=0),
        name="inner_transport",
    )(own, before, after, spread)
    return pl.pallas_call(
        outer_kernel,
        out_shape=(
            jax.ShapeDtypeStruct((SPECIES, CX, CY), F32),
            jax.ShapeDtypeStruct((CX, CY), F32),
        ),
        in_specs=[SMEM] * 2 + [VMEM] * 12,
        out_specs=(pl.BlockSpec(memory_space=pltpu.HBM),) * 2,
        scratch_shapes=[
            pltpu.VMEM((CX + 18, FT, 8, WIDE), F32),
            pltpu.VMEM((2, CX + 18, 8, WIDE), F32),
            pltpu.VMEM((44, FT, 8, WIDE), F32),
            pltpu.VMEM((38, FT, 8, WIDE), F32),
            pltpu.VMEM((TILES, FT, 8, 128), F32),
            pltpu.VMEM((TILES * ROWS, 128), F32),
            pltpu.VMEM((SPECIES, CX, CY), F32),
            pltpu.VMEM((CX, CY), F32),
            pltpu.SemaphoreType.DMA((CX // 8 + 1,)),
        ],
        compiler_params=pltpu.CompilerParams(vmem_limit_bytes=36 * 2**20),
        name="outer_transport_and_chemistry",
    )(counts, rank, above, own, before, after, below, one, two, tiles, spread, gathers, sums, warm)


def solution(mesh):
    return jax.shard_map(
        body,
        mesh=mesh,
        in_specs=(
            P(None, "gx", "grp"),
            P("gx", "grp"),
            P("gx", "grp"),
            P("gx", "grp"),
            P(),
            P(),
            P(),
            P(),
            P(),
            P(),
            P(("grp", "gx")),
        ),
        out_specs=(P(None, "gx", "grp"), P("gx", "grp")),
        check_vma=False,
    )
```

```python
import functools
import math

import jax
import jax.numpy as jnp
from jax import lax
from jax.experimental import pallas as pl
from jax.experimental.pallas import tpu as pltpu
from jax.sharding import PartitionSpec as P

SPECIES = 53
ROWS = 56
FT = ROWS // 8
CX, CY = 32, 256
TILES = 64
HALO = 9
WIDE = 384
RXN = 336
GROUP = 8
CELLS = GROUP * 128
DT = 0.4
SPAN = 0.5
FIRST = (0.75, -0.15, 1.0 / 60.0)
CENTER = -49.0 / 18.0
FLOOR = 1e-20
F32, BF16 = jnp.float32, jnp.bfloat16


def two_parts(value):
    high = value.astype(BF16).astype(F32)
    return high, value - high


def pack_kernel(
    density_hbm,
    thermal_hbm,
    lead_hbm,
    trail_hbm,
    own_hbm,
    first,
    last,
    left_hbm,
    right_hbm,
    density,
    others,
    own,
    left_edges,
    right_edges,
    sems,
    out_sems,
):
    copies = []
    for b in range(CX // 8):
        at = slice(b * 8, b * 8 + 8)
        now = [pltpu.make_async_copy(density_hbm.at[:, at], density.at[:, at], sems.at[b, 0])]
        for i, source in enumerate((thermal_hbm, lead_hbm, trail_hbm)):
            now.append(pltpu.make_async_copy(source.at[at], others.at[i, at], sems.at[b, 1 + i]))
        copies.append(now)
    for now in copies:
        for copy in now:
            copy.start()
    lane = lax.broadcasted_iota(jnp.int32, (8, 128), 1)
    rows = own.reshape(CX, 14, 8, 128)
    ends = []

    def send(source, target):
        ends.append(pltpu.make_async_copy(source, target, out_sems.at[len(ends)]))
        ends[-1].start()

    for b in range(CX // 8):
        for copy in copies[b]:
            copy.wait()
        for half in range(2):
            for f in range(ROWS):
                source, i = (density, f) if f < SPECIES else (others, f - SPECIES)
                value = source[i, b * 8 : b * 8 + 8, half * 128 : half * 128 + 128]
                row = (b * 8 * 14 + 2 * (f // 8) + half) * 8 + f % 8
                own[pl.ds(row, 8, stride=14 * 8), :] = value
        if b == 1:
            send(rows.at[:HALO], first.at[:, :14])
            send(rows.at[: CX // 2], own_hbm.at[: CX // 2])
        if b == 3:
            send(rows.at[CX - HALO :], last.at[:, :14])
            send(rows.at[CX // 2 :], own_hbm.at[CX // 2 :])
    for x in range(CX // 2):
        sides = []
        for edge, places in ((0, (0, 63)), (119, (63, 0))):
            packed = jnp.zeros((8, 128), F32)
            for y, place in zip((x, x + CX // 2), places):
                for t in range(FT):
                    row = (y * 14 + 2 * t + (edge > 0)) * 8
                    at = place + 9 * t
                    turned = pltpu.roll(own[row : row + 8, :], (at - edge) % 128, 1)
                    packed = jnp.where((lane >= at) & (lane < at + HALO), turned, packed)
            sides.append(packed)
        left_edges[x], right_edges[x] = sides
    send(left_edges, left_hbm)
    send(right_edges, right_hbm)
    for copy in ends:
        copy.wait()


def stage_block(b, src, base, base_at, diffusion, speeds, speed_at, starts, block, mix, store):
    keep, take = mix
    for t, start in ((t, start) for t in range(FT) for start in starts):
        x0 = start + b * block
        r = jnp.concatenate([diffusion[t]] * 3, axis=1)
        pull = [(2.0 / k) * r for k in (1, 2, 3)]
        rc = (2.0 * DT * CENTER) * r
        f = [src[x0 + i, t] for i in range(block + 6)]
        q = [speeds[0, speed_at + x0 + i] * f[i] for i in range(block + 6)]
        for i in range(block):
            j = i + 3
            v = speeds[1, speed_at + x0 + j] * f[j]
            total = rc * f[j]
            for k in (1, 2, 3):
                even = pull[k - 1] * f[j]
                turned = pltpu.roll(even - v, WIDE - k, 1) + pltpu.roll(even + v, k, 1)
                along = pull[k - 1] * (f[j + k] + f[j - k]) - (q[j + k] - q[j - k])
                total = total + (DT * FIRST[k - 1]) * (turned + along)
            out = f[j] + total
            if keep is not None:
                out = keep * base[base_at + x0 + i, t] + take * out
            store(x0 + i, t, out)


def run_stage(src, base, base_at, diffusion, speeds, speed_at, starts, rows, block, mix, store):
    def at_block(b, _):
        stage_block(b, src, base, base_at, diffusion, speeds, speed_at, starts, block, mix, store)
        return 0

    lax.fori_loop(0, rows // block, at_block, 0)


def react_group(g, counts, order, tiles, gathers, sums, warming, done, beside=()):
    ids = [order[g * GROUP + i] for i in range(GROUP)]
    per_tile = [counts[i] for i in ids]
    number = jnp.concatenate([jnp.full((1, 128), n, jnp.int32) for n in per_tile], axis=1)
    h = SPAN / number.astype(F32)
    row = lax.broadcasted_iota(jnp.int32, (ROWS, CELLS), 0)
    species = row < SPECIES
    state = jnp.concatenate([tiles[i].reshape(ROWS, 128) for i in ids], axis=1)
    state = jnp.where(species, jnp.maximum(state, 0.0), state)

    def tail(value, a, b, c):
        a = jnp.where(row == SPECIES, a, jnp.where(row == SPECIES + 1, b, c))
        return jnp.where(species, value, a)

    def advance(s, state):
        w = state[SPECIES : SPECIES + 1]
        safe = jnp.maximum(state, FLOOR)
        high, rest = two_parts(jnp.log2(safe))
        middle, low = two_parts(rest)
        heat = jnp.tanh(w)
        heat_0, rest = two_parts(heat)
        heat_1, heat_2 = two_parts(rest)
        stacked = jnp.concatenate(
            [
                tail(high, heat_0, heat_1, 1.0),
                tail(middle, heat_0, 1.0, 1.0),
                tail(low, heat_1, heat_2, heat_0),
            ],
            axis=0,
        ).astype(BF16)
        p = jnp.exp2(jnp.dot(gathers[...], stacked, preferred_element_type=F32))
        high, low = two_parts(p)
        both = jnp.concatenate([high, low], axis=0).astype(BF16)
        totals = jnp.dot(sums[...], both, preferred_element_type=F32)
        gained = totals[:ROWS] + totals[ROWS : 2 * ROWS]
        lost = totals[2 * ROWS : 3 * ROWS]
        updated = safe * (state + h * gained) / (safe + h * lost)
        warm = jnp.concatenate([warming[...]] * GROUP, axis=1)
        rise = jnp.where(species, warm * (updated - state), 0.0)
        warmer = w + jnp.sum(rise, axis=0, keepdims=True)
        after = jnp.where(species, updated, jnp.broadcast_to(warmer, (ROWS, CELLS)))
        return jnp.where(s < number, after, state)

    turns = functools.reduce(jnp.maximum, per_tile)
    if beside:
        turns_beside, work = beside

        def both(s, state):
            work(s)
            return advance(s, state)

        state = lax.fori_loop(0, turns_beside, both, state)
        state = lax.fori_loop(turns_beside, turns, advance, state)
    else:
        state = lax.fori_loop(0, turns, advance, state)
    for i in range(GROUP):
        place = (ids[i] & 1) * CX + (ids[i] >> 1)
        at = pl.multiple_of(place * ROWS, 8)
        done[pl.ds(at, ROWS), :] = state[:, i * 128 : i * 128 + 128]


def widen(slab, speeds, at, tiles_of, after, before, after_at, before_at):
    lane = lax.broadcasted_iota(jnp.int32, (8, 128), 1)
    for t in range(FT):
        right = pltpu.roll(after, (-after_at - 9 * t) % 128, 1)
        left = pltpu.roll(before, (119 - before_at - 9 * t) % 128, 1)
        tile = jnp.where(lane < HALO, right, jnp.where(lane >= 128 - HALO, left, 0.0))
        value = jnp.concatenate([tiles_of(2 * t), tiles_of(2 * t + 1), tile], axis=1)
        slab[at, t] = value
        if t == FT - 1:
            speeds[0, at] = jnp.broadcast_to(value[6:7], (8, WIDE))
            speeds[1, at] = jnp.broadcast_to(value[7:8], (8, WIDE))


def put(target, shift=0):
    def store(x, t, value):
        target[x + shift, t] = value

    return store


def put_tiles(target, shift=0):
    def store(x, t, value):
        target[2 * (x + shift), t] = value[:, :128]
        target[2 * (x + shift) + 1, t] = value[:, 128:256]

    return store


SECOND_MIX, THIRD_MIX = (0.75, 0.25), (1.0 / 3.0, 2.0 / 3.0)


def inner_kernel(own, before, after, diffusion, one_out, two_out, tiles, slab, speeds, one, two):
    def at_row(x, _):
        y = x + CX // 2
        widen(slab, speeds, x, lambda j: own[x, j], after[x], before[x], 0, 63)
        widen(slab, speeds, y, lambda j: own[y, j], after[x], before[x], 63, 0)
        return 0

    lax.fori_loop(0, CX // 2, at_row, 0, unroll=8)
    run_stage(slab, None, 0, diffusion, speeds, 0, (0,), 26, 13, (None, None), put(one))
    run_stage(one, slab, 6, diffusion, speeds, 3, (0,), 20, 10, SECOND_MIX, put(two))
    run_stage(two, slab, 9, diffusion, speeds, 6, (0,), 14, 7, THIRD_MIX, put_tiles(tiles))
    for i in range(6):
        one_out[i] = one[i]
        one_out[6 + i] = one[20 + i]
        two_out[i] = two[i]
        two_out[6 + i] = two[14 + i]


def outer_kernel(
    counts,
    order,
    above,
    own,
    before,
    after,
    below,
    one_in,
    two_in,
    tiles_in,
    diffusion,
    gathers,
    sums,
    warming,
    species_hbm,
    warmth_hbm,
    slab,
    speeds,
    one,
    two,
    tiles,
    done,
    species_out,
    warmth_out,
    sems,
):
    def at_row(x, _):
        widen(slab, speeds, x, lambda j: above[x, j], above[x, 14], above[x, 14], 63, 0)
        widen(slab, speeds, HALO + CX + x, lambda j: below[x, j], below[x, 14], below[x, 14], 0, 63)
        return 0

    def at_own_row(x, _):
        y, z = CX - 12 + x, CX // 2 - 12 + x
        widen(slab, speeds, HALO + x, lambda j: own[x, j], after[x], before[x], 0, 63)
        widen(slab, speeds, HALO + y, lambda j: own[y, j], after[z], before[z], 63, 0)
        return 0

    lax.fori_loop(0, HALO, at_row, 0, unroll=9)
    lax.fori_loop(0, 12, at_own_row, 0, unroll=6)
    for i in range(6):
        one[9 + i] = one_in[i]
        one[29 + i] = one_in[6 + i]
        two[9 + i] = two_in[i]
        two[23 + i] = two_in[6 + i]
    tiles[18:46] = tiles_in[...]
    args = (diffusion, speeds)
    stages = (
        (slab, None, 0, *args, 0, (0, 35), 9, (None, None), put(one)),
        (one, slab, 6, *args, 3, (0, 29), 9, SECOND_MIX, put(two)),
        (two, slab, 9, *args, 6, (0, 23), 9, THIRD_MIX, put_tiles(tiles)),
    )
    mechanism = (counts, order, tiles, gathers, sums, warming, done)
    for g, stage in enumerate(stages):
        react_group(g, *mechanism, beside=(1, lambda b: stage_block(b, *stage)))

    def at_group(g, _):
        react_group(g, *mechanism)
        return 0

    lax.fori_loop(3, TILES // GROUP, at_group, 0)

    copies = []
    for b in range(CX // 8):
        at = slice(b * 8, b * 8 + 8)
        for half in range(2):
            lanes = slice(half * 128, half * 128 + 128)
            row = (half * CX + b * 8) * ROWS
            for s in range(SPECIES):
                species_out[s, at, lanes] = done[pl.ds(row + s, 8, stride=ROWS), :]
            warmth_out[at, lanes] = done[pl.ds(row + SPECIES, 8, stride=ROWS), :]
        copies.append(pltpu.make_async_copy(species_out.at[:, at], species_hbm.at[:, at], sems.at[b]))
        copies[-1].start()
    copies.append(pltpu.make_async_copy(warmth_out, warmth_hbm, sems.at[CX // 8]))
    copies[-1].start()
    for copy in copies:
        copy.wait()


def parts(value, number):
    out = []
    for _ in range(number):
        out.append(lax.reduce_precision(value, 8, 7))
        value = value - out[-1]
    return out


def fetch_kernel(source, own):
    own[...] = source[...]


def tables(pairs, exponents, energies, output, diffusion, warming):
    extra = RXN - pairs.shape[0]
    padded = jnp.pad(pairs, ((0, extra), (0, 0)), constant_values=-1).T
    row = jnp.arange(3 * ROWS, dtype=jnp.int32)[:, None]
    ids = row % ROWS
    taken = (padded[:1] == ids).astype(F32) + (padded[1:] == ids).astype(F32)
    scale = 1.0 / math.log(2.0)
    a = parts(jnp.pad(scale * exponents, (0, extra)), 3)
    e = parts(jnp.pad(scale * energies, (0, extra)), 3)
    gathers = taken
    for i, tail in enumerate(((e[0], e[0], a[0]), (e[1], a[1], a[2]), (e[1], e[0], e[2]))):
        for j, value in enumerate(tail):
            gathers = jnp.where(row == i * ROWS + SPECIES + j, value[None], gathers)
    gathers = gathers.T
    high, low = parts(jnp.pad(output, ((0, extra), (0, ROWS - SPECIES))).T, 2)
    sums = jnp.concatenate([high, low, taken[:ROWS], jnp.zeros((8, RXN), F32)], 0)
    sums = jnp.concatenate([sums, sums], 1)

    def column(values):
        values = jnp.pad(values, (0, ROWS - values.shape[0]))
        return jnp.broadcast_to(values[:, None], (ROWS, 128))

    return (column(diffusion).reshape(FT, 8, 128), gathers.astype(BF16), sums.astype(BF16), column(warming))


def ranked(counts):
    number = jnp.arange(TILES, dtype=jnp.int32)
    outer = jnp.where((number >= 18) & (number < 46), 0, 8 * TILES)
    key = outer + counts * TILES + number
    rank = jnp.sum((key[None, :] < key[:, None]).astype(jnp.int32), axis=1)
    rank = jnp.where(rank < 28, (rank + 24) % 28, rank)
    return jnp.sum(jnp.where(rank[None, :] == number[:, None], number[None, :], 0), axis=1)


def neighbours(axis):
    n = lax.axis_size(axis)
    up = [(i, (i + 1) % n) for i in range(n)]
    return up, [(j, i) for i, j in up]


VMEM = pl.BlockSpec(memory_space=pltpu.VMEM)
SMEM = pl.BlockSpec(memory_space=pltpu.SMEM)


def body(density, thermal, lead, trail, diffusion, pairs, exponents, energies, output, warming, counts):
    own, first, last, left, right = pl.pallas_call(
        pack_kernel,
        out_shape=(
            jax.ShapeDtypeStruct((CX, 14, 8, 128), F32),
            jax.ShapeDtypeStruct((HALO, 15, 8, 128), F32),
            jax.ShapeDtypeStruct((HALO, 15, 8, 128), F32),
            jax.ShapeDtypeStruct((CX // 2, 8, 128), F32),
            jax.ShapeDtypeStruct((CX // 2, 8, 128), F32),
        ),
        in_specs=[pl.BlockSpec(memory_space=pltpu.HBM)] * 4,
        out_specs=(pl.BlockSpec(memory_space=pltpu.HBM),) * 5,
        scratch_shapes=[
            pltpu.VMEM((SPECIES, CX, CY), F32),
            pltpu.VMEM((3, CX, CY), F32),
            pltpu.VMEM((CX * 112, 128), F32),
            pltpu.VMEM((CX // 2, 8, 128), F32),
            pltpu.VMEM((CX // 2, 8, 128), F32),
            pltpu.SemaphoreType.DMA((CX // 8, 4)),
            pltpu.SemaphoreType.DMA((6,)),
        ],
        compiler_params=pltpu.CompilerParams(vmem_limit_bytes=55 * 2**20),
        name="pack",
    )(density, thermal, lead, trail)
    up, down = neighbours("grp")
    before = lax.ppermute(right, "grp", up)
    after = lax.ppermute(left, "grp", down)
    consts = tables(pairs, exponents, energies, output, diffusion, warming)
    own = pl.pallas_call(
        fetch_kernel,
        out_shape=jax.ShapeDtypeStruct((CX, 14, 8, 128), F32),
        in_specs=[VMEM],
        out_specs=VMEM,
        compiler_params=pltpu.CompilerParams(vmem_limit_bytes=16 * 2**20),
        name="fetch",
    )(own)
    before, after, own, rank, (spread, gathers, sums, warm) = lax.optimization_barrier(
        (before, after, own, ranked(counts), consts)
    )
    side = jnp.arange(128, dtype=jnp.int32) < 63
    first = first.at[:, 14].set(jnp.where(side, after[:HALO], before[:HALO]))
    last = last.at[:, 14].set(jnp.where(side, before[-HALO:], after[-HALO:]))
    up, down = neighbours("gx")
    above = lax.ppermute(last, "gx", up)
    below = lax.ppermute(first, "gx", down)
    one, two, tiles = pl.pallas_call(
        inner_kernel,
        out_shape=(
            jax.ShapeDtypeStruct((12, FT, 8, WIDE), F32),
            jax.ShapeDtypeStruct((12, FT, 8, WIDE), F32),
            jax.ShapeDtypeStruct((28, FT, 8, 128), F32),
        ),
        in_specs=[VMEM] * 4,
        out_specs=(VMEM,) * 3,
        scratch_shapes=[
            pltpu.VMEM((CX, FT, 8, WIDE), F32),
            pltpu.VMEM((2, CX, 8, WIDE), F32),
            pltpu.VMEM((26, FT, 8, WIDE), F32),
            pltpu.VMEM((20, FT, 8, WIDE), F32),
        ],
        compiler_params=pltpu.CompilerParams(vmem_limit_bytes=20 * 2**20),
        cost_estimate=pl.CostEstimate(flops=10**9, bytes_accessed=30 * 10**6, transcendentals=0),
        name="inner_transport",
    )(own, before, after, spread)
    return pl.pallas_call(
        outer_kernel,
        out_shape=(
            jax.ShapeDtypeStruct((SPECIES, CX, CY), F32),
            jax.ShapeDtypeStruct((CX, CY), F32),
        ),
        in_specs=[SMEM] * 2 + [VMEM] * 12,
        out_specs=(pl.BlockSpec(memory_space=pltpu.HBM),) * 2,
        scratch_shapes=[
            pltpu.VMEM((CX + 18, FT, 8, WIDE), F32),
            pltpu.VMEM((2, CX + 18, 8, WIDE), F32),
            pltpu.VMEM((44, FT, 8, WIDE), F32),
            pltpu.VMEM((38, FT, 8, WIDE), F32),
            pltpu.VMEM((TILES, FT, 8, 128), F32),
            pltpu.VMEM((TILES * ROWS, 128), F32),
            pltpu.VMEM((SPECIES, CX, CY), F32),
            pltpu.VMEM((CX, CY), F32),
            pltpu.SemaphoreType.DMA((CX // 8 + 1,)),
        ],
        compiler_params=pltpu.CompilerParams(vmem_limit_bytes=36 * 2**20),
        name="outer_transport_and_chemistry",
    )(counts, rank, above, own, before, after, below, one, two, tiles, spread, gathers, sums, warm)


def solution(mesh):
    return jax.shard_map(
        body,
        mesh=mesh,
        in_specs=(
            P(None, "gx", "grp"),
            P("gx", "grp"),
            P("gx", "grp"),
            P("gx", "grp"),
            P(),
            P(),
            P(),
            P(),
            P(),
            P(),
            P(("grp", "gx")),
        ),
        out_specs=(P(None, "gx", "grp"), P("gx", "grp")),
        check_vma=False,
    )
```
